256 devices in a mesh: layer: 32 (over x, y, core), dp: 8 (over z).
Axes of the slice: x: 4, y: 4, z: 8, core: 2. Of those that a mesh axis runs over, the one named last changes fastest.
Arguments:
- embedded: float32 [1024, 1024], P('dp'), may hold values from -6 to 6
- guess: float32 [32, 1024, 1024], P('layer', 'dp'), may hold values from -12 to 12
- qkv_weight: bfloat16 [32, 1024, 3072], P('layer')
- out_weight: bfloat16 [32, 1024, 1024], P('layer'), may hold values from -0.1875 to 0.1875
- norm_gain: float32 [32, 1024], P('layer'), may hold values from 0.1 to 1.9
- cotangent: float32 [1024, 1024], P('dp'), may hold values from -6 to 6
- adjoint_guess: float32 [32, 1024, 1024], P('layer', 'dp'), may hold values from -6 to 6
Outputs:
- states: float32 [32, 1024, 1024], P('layer', 'dp')
- adjoints: float32 [32, 1024, 1024], P('layer', 'dp')
- gain_grads: float32 [32, 1024], P('layer')
The draws below stay inside these ranges and needn't reach their ends.
All inputs are finite; a program needn't handle non-finite values.
Results may differ from the reference program's by a relative error of at most 0.04.
Values sent between devices are 32-bit elements; how exact they have to be, the bound alone decides.
A program may use at most 64 MiB of HBM per device.

```python
import jax
import jax.numpy as jnp
from jax import lax

D = 1024
HEADS = 8
SEQ = 128
CYCLES = 2
TOKENS = 1024
LAYERS = 32


def draw_qkv_weight(key, part):
    key = jax.random.fold_in(key, 17)
    base_key = jax.random.fold_in(key, 0)
    full_shape = (LAYERS, D, 3 * D)
    return (jnp.clip(jax.random.normal(base_key, full_shape, jnp.float32), -4.0, 4.0) * D ** (-0.5)).astype(jnp.bfloat16)


def levels(own_key, shape, cuts, least, largest):
    gain = 1.0
    for axis_at, shards_of in cuts:
        draws = jax.random.uniform(jax.random.fold_in(jax.random.fold_in(own_key, 6), axis_at), (shards_of,), jnp.float32, least / len(cuts), largest / len(cuts))
        gain = gain * jnp.repeat(jnp.exp(draws), shape[axis_at] // shards_of).reshape((-1,) + (1,) * (len(shape) - 1 - axis_at))
    return gain


def noise(own_key, dims, width, reach, shards=(), kind=jnp.bfloat16):
    entries = jax.random.normal(own_key, dims, jnp.float32) * width
    if len(shards) > 0:
        entries = levels(own_key, dims, shards, -0.22, 0.18) * entries
    return jnp.clip(entries, min=-reach, max=reach).astype(kind)


def setup_inputs(seed: int = 0) -> dict:
    splits = jax.random.split(jax.random.key(seed), 8)
    return {
        "embedded": noise(splits[0], (TOKENS, D), 1.0, 6.0, ((0, 8),), jnp.float32),
        "guess": noise(splits[1], (LAYERS, TOKENS, D), 2.0, 12.0, ((0, 32), (1, 8)), jnp.float32),
        "qkv_weight": draw_qkv_weight(jax.random.fold_in(splits[7], 71), 0),
        "out_weight": noise(splits[3], (LAYERS, D, D), D ** -0.5, 0.1875, ((0, 32),)),
        "norm_gain": jnp.clip(1.0 + 0.18 * jax.random.normal(splits[4], (LAYERS, D), jnp.float32), 0.1, 1.9),
        "cotangent": noise(splits[5], (TOKENS, D), 1.0, 6.0, ((0, 8),), jnp.float32),
        "adjoint_guess": noise(splits[6], (LAYERS, TOKENS, D), 1.0, 6.0, ((0, 32), (1, 8)), jnp.float32),
    }


coarse_ratio = 4.0
norm_eps = 1e-06

def attend(stream, w_qkv, w_out, gain_vec):
    row_count, feat_width = stream.shape
    head_dim = feat_width // HEADS
    square = lax.optimization_barrier(jnp.mean(stream * stream, axis=-1, keepdims=True))
    normed = (stream * lax.rsqrt(square + norm_eps) * gain_vec).astype(jnp.bfloat16)
    projected = jnp.dot(normed, w_qkv, preferred_element_type=jnp.float32).astype(jnp.bfloat16)
    blocks = row_count // SEQ
    projected = projected.reshape(blocks, SEQ, 3, HEADS, head_dim).astype(jnp.float32)
    queries, key_rows, value_rows = (projected[:, :, 0], projected[:, :, 1], projected[:, :, 2])
    scores = jnp.einsum('bqhd,bkhd->bhqk', queries, key_rows) / head_dim ** 0.5
    causal = lax.broadcasted_iota(jnp.int32, (SEQ, SEQ), 0) >= lax.broadcasted_iota(jnp.int32, (SEQ, SEQ), 1)
    scores = jnp.where(causal, scores, -1e+30)
    highest = lax.optimization_barrier(jnp.max(scores, axis=-1, keepdims=True))
    exponent = jnp.exp(scores - highest)
    attn_probs = (exponent / lax.optimization_barrier(jnp.sum(exponent, axis=-1, keepdims=True))).astype(jnp.bfloat16)
    context = jnp.einsum('bhqk,bkhd->bqhd', attn_probs.astype(jnp.float32), value_rows).astype(jnp.bfloat16)
    return jnp.dot(context.reshape(row_count, feat_width), w_out, preferred_element_type=jnp.float32)

def advance(stream, w_qkv, w_out, gain_vec):
    return stream + attend(stream, w_qkv, w_out, gain_vec)

def relax(sections):

    def run_group(pieces):
        stream, w_qkv, w_out, gains = pieces
        results = []
        for section_num in range(sections):
            stream = advance(stream, w_qkv[section_num], w_out[section_num], gains[section_num])
            results.append(stream)
        return jnp.stack(results)
    return run_group

def reference(embedded, guess, qkv_weight, out_weight, norm_gain, cotangent, adjoint_guess):
    groups = LAYERS // 4

    def by_group(array):
        return array.reshape((groups, 4) + array.shape[1:])
    qkv_groups = by_group(qkv_weight)
    out_groups = by_group(out_weight)
    gain_groups = by_group(norm_gain)
    current = guess
    for cycle_num in range(CYCLES):
        before = jnp.concatenate([embedded[None], current[:-1]], axis=0)
        starts = before[0::4]
        fine = lax.map(relax(4), (starts, qkv_groups, out_groups, gain_groups))
        ends = fine[:, 3]

        def coarse_step(value, pieces):
            start, end, w_qkv, w_out, gains = pieces
            change = value - start + coarse_ratio * (attend(value, w_qkv, w_out, gains) - attend(start, w_qkv, w_out, gains))
            solved = end + change
            return (solved, solved)
        _, solved = lax.scan(coarse_step, embedded, (starts, ends, qkv_groups[:, 3], out_groups[:, 3], gain_groups[:, 3]))
        new_starts = jnp.concatenate([embedded[None], solved[:-1]], axis=0)
        inner = lax.map(relax(3), (new_starts, qkv_groups, out_groups, gain_groups))
        current = jnp.concatenate([inner, solved[:, None]], axis=1).reshape(guess.shape)
    inputs = jnp.concatenate([embedded[None], current[:-1]], axis=0)
    after = jnp.concatenate([adjoint_guess[1:], cotangent[None]], axis=0)

    def backward(pieces):
        layer_in, received, w_qkv, w_out, gains = pieces
        adjoint_list = [None, None, None, None]
        grad_list = [None, None, None, None]
        for section_num in range(3, -1, -1):
            _, puller = jax.vjp(lambda stream, gain_vec: advance(stream, w_qkv[section_num], w_out[section_num], gain_vec), layer_in[section_num], gains[section_num])
            received, grad_list[section_num] = puller(received)
            adjoint_list[section_num] = received
        return (jnp.stack(adjoint_list), jnp.stack(grad_list))
    adjoint_all, grad_all = lax.map(backward, (by_group(inputs), after[3::4], qkv_groups, out_groups, gain_groups))
    return (current, adjoint_all.reshape(adjoint_guess.shape), grad_all.reshape(norm_gain.shape))
```

```python
import functools

import jax
import jax.numpy as jnp
from jax import lax
from jax.experimental import pallas as pl
from jax.experimental.pallas import tpu as pltpu
from jax.sharding import PartitionSpec as P

HEADS = 8
SEQ = 128
ROWS = 32
PASSES = 6

coarse_ratio = 4.0
norm_eps = 1e-06

F32 = jnp.float32
BF16 = jnp.bfloat16
MESH = pl.DeviceIdType.MESH


def dot(a, b):
    return jnp.dot(a, b, preferred_element_type=F32)


def dot_nt(a, b):
    return lax.dot_general(a, b, (((1,), (1,)), ((), ())), preferred_element_type=F32)


def dot_tn(a, b):
    return lax.dot_general(a, b, (((0,), (0,)), ((), ())), preferred_element_type=F32)


def kernel(
    depth,
    copies,
    embedded,
    guess,
    qkv_weight,
    out_weight,
    gain,
    cotangent,
    adjoint_guess,
    states,
    adjoints,
    grads,
    w_qkv,
    w_out,
    ins,
    outs,
    base,
    proj,
    probs,
    context,
    received,
    returned,
    d_kv,
    gain_parts,
    weight_sem,
    in_sem,
    out_sem,
    far_sem,
    guess_sem,
    back_in_sem,
    back_out_sem,
    gain_in_sem,
    gain_out_sem,
    final_sem,
):
    width = gain.shape[-1]
    head_dim = width // HEADS
    chunks = SEQ // ROWS
    groups = depth // 4
    me = lax.axis_index("layer")
    replica = lax.axis_index("dp")
    group = me // 4
    within = me % 4
    last_group = group == groups - 1
    following = lax.rem(me + 1, depth)
    preceding = lax.rem(me + depth - 1, depth)
    far_on = lax.rem(me + 4, depth)
    far_back = lax.rem(me + depth - 4, depth)

    barrier = pltpu.get_barrier_semaphore()
    for neighbour in (following, preceding):
        pl.semaphore_signal(
            barrier, inc=1, device_id={"layer": neighbour}, device_id_type=MESH
        )
    for offset in range(1, copies):
        pl.semaphore_signal(
            barrier,
            inc=1,
            device_id={"dp": lax.rem(replica + offset, copies)},
            device_id_type=MESH,
        )

    @pl.when(within == 3)
    def _():
        for neighbour in (far_on, far_back):
            pl.semaphore_signal(
                barrier, inc=1, device_id={"layer": neighbour}, device_id_type=MESH
            )

    load_qkv = pltpu.make_async_copy(qkv_weight.at[0], w_qkv, weight_sem.at[0])
    load_out = pltpu.make_async_copy(out_weight.at[0], w_out, weight_sem.at[1])
    load_qkv.start()
    load_out.start()

    def rows_of(chunk):
        return pl.ds(pl.multiple_of(chunk * ROWS, ROWS), ROWS)

    def embed_copy(chunk):
        return pltpu.make_async_copy(
            embedded.at[rows_of(chunk)], ins.at[1, rows_of(chunk)], in_sem.at[1, chunk]
        )

    def cotangent_copy(chunk):
        return pltpu.make_async_copy(
            cotangent.at[rows_of(chunk)], received.at[rows_of(chunk)], back_in_sem.at[chunk]
        )

    @pl.when(me == 0)
    def _():
        for chunk in range(chunks):
            embed_copy(chunk).start()

    @pl.when(me == depth - 1)
    def _():
        for chunk in range(chunks):
            cotangent_copy(chunk).start()

    proj[...] = jnp.zeros_like(proj)
    base[...] = jnp.zeros_like(base)
    d_kv[...] = jnp.zeros_like(d_kv)

    pl.semaphore_wait(barrier, copies + 1 + 2 * (within // 3))

    def send_guess(chunk, place, target):
        return pltpu.make_async_remote_copy(
            src_ref=guess.at[0, rows_of(chunk)],
            dst_ref=ins.at[place, rows_of(chunk)],
            send_sem=guess_sem.at[place, chunk],
            recv_sem=in_sem.at[place, chunk],
            device_id={"layer": target},
            device_id_type=MESH,
        )

    def send_adjoint_guess(chunk):
        return pltpu.make_async_remote_copy(
            src_ref=adjoint_guess.at[0, rows_of(chunk)],
            dst_ref=received.at[rows_of(chunk)],
            send_sem=back_out_sem.at[chunk],
            recv_sem=back_in_sem.at[chunk],
            device_id={"layer": preceding},
            device_id_type=MESH,
        )

    gives_guess = (within == 3) & (group < groups - 1)
    gives_adjoint_guess = (within == 0) & (group > 0)

    @pl.when(gives_guess)
    def _():
        for chunk in range(chunks):
            send_guess(chunk, 1, following).start()
        for chunk in range(chunks):
            send_guess(chunk, 0, far_on).start()

    @pl.when(gives_adjoint_guess)
    def _():
        for chunk in range(chunks):
            send_adjoint_guess(chunk).start()

    load_qkv.wait()
    load_out.wait()

    def send_next(place, chunk, to_place):
        return pltpu.make_async_remote_copy(
            src_ref=outs.at[place, rows_of(chunk)],
            dst_ref=ins.at[to_place, rows_of(chunk)],
            send_sem=out_sem.at[place, chunk],
            recv_sem=in_sem.at[to_place, chunk],
            device_id={"layer": following},
            device_id_type=MESH,
        )

    def send_far(place, chunk, to_place):
        return pltpu.make_async_remote_copy(
            src_ref=outs.at[place, rows_of(chunk)],
            dst_ref=ins.at[to_place, rows_of(chunk)],
            send_sem=far_sem.at[place, chunk],
            recv_sem=in_sem.at[to_place, chunk],
            device_id={"layer": far_on},
            device_id_type=MESH,
        )

    def is_active(place):
        needed = jnp.where(place == 0, 1, place // 2)
        return ((within == 3) | (place % 2 == 1)) & (group >= needed)

    def relays_fine(place):
        return is_active(place) & (within < 3)

    def relays_first(place):
        right = ((group == 0) & (place == 1)) | ((group >= 1) & (place == 2))
        return (within == 3) & (group < groups - 1) & right

    def relays_second(place):
        right = ((group == 1) & (place == 3)) | ((group >= 2) & (place == 4))
        return (within == 3) & (group < groups - 1) & right

    causal_cols = lax.broadcasted_iota(jnp.int32, (ROWS, SEQ), 1)
    causal_rows = lax.broadcasted_iota(jnp.int32, (ROWS, SEQ), 0)
    scale = head_dim**-0.5

    def forward(place, chunk):
        rows = rows_of(chunk)
        parity = place % 2
        pltpu.make_async_copy(
            ins.at[place, rows], ins.at[place, rows], in_sem.at[place, chunk]
        ).wait()
        stream = ins[place, rows, :]
        square = jnp.sum(stream * stream, axis=-1, keepdims=True) * (1.0 / width)
        root = lax.rsqrt(square + norm_eps)
        scaled = (stream * gain[...]).astype(BF16)
        proj[parity, rows, :] = (dot(scaled, w_qkv[...]) * root).astype(BF16)
        causal = causal_rows + chunk * ROWS >= causal_cols
        scores = []
        for head in range(HEADS):
            first = head * head_dim
            query = proj[parity, rows, first : first + head_dim]
            key = proj[parity, :, width + first : width + first + head_dim]
            scores.append(jnp.where(causal, dot_nt(query, key) * scale, -1e30))
        exps = [jnp.exp(s - jnp.max(s, axis=-1, keepdims=True)) for s in scores]
        inverses = [1.0 / jnp.sum(e, axis=-1, keepdims=True) for e in exps]
        for head in range(HEADS):
            first = head * head_dim
            value = proj[parity, :, 2 * width + first : 2 * width + first + head_dim]
            mixed = dot(exps[head].astype(BF16), value) * inverses[head]
            context[:, first : first + head_dim] = mixed.astype(BF16)
            probs[parity, head, rows, :] = (exps[head] * inverses[head]).astype(BF16)

        @pl.when((within < 3) | (place < 5))
        def _():
            odd = place % 2 == 1
            ratio = jnp.where(odd, 1.0, coarse_ratio)
            mix = dot(context[...], w_out[...])
            step = ins[place, rows, :] + ratio * mix
            old = base[rows, :]
            with_old = jnp.where((place == 2) | (place == 4), 1.0, 0.0)
            outs[place, rows, :] = step + with_old * old

            @pl.when(relays_fine(place))
            def _():
                send_next(place, chunk, place).start()

            @pl.when(relays_first(place))
            def _():
                send_far(place, chunk, 2).start()
                send_next(place, chunk, 3).start()

            @pl.when(relays_second(place))
            def _():
                send_far(place, chunk, 4).start()
                send_next(place, chunk, 5).start()

            base[rows, :] = jnp.where(odd, old + step, -step)

    def one_task(task, carry):
        mixed = task - 3 * chunks
        early = task < 3 * chunks
        late = task >= 5 * chunks
        place = jnp.where(early, task // chunks, jnp.where(late, 5, 3 + mixed % 2))
        chunk = jnp.where(
            early, task % chunks, jnp.where(late, task - 5 * chunks, mixed // 2)
        )

        @pl.when(is_active(place))
        def _():
            forward(place, chunk)

        return carry

    lax.fori_loop(0, PASSES * chunks, one_task, 0)

    latest = 1 + 2 * jnp.minimum(group, 2)
    final = latest - jnp.where((within == 3) & (group >= 2), 1, 0)
    write_states = pltpu.make_async_copy(outs.at[final], states.at[0], final_sem.at[0])
    write_states.start()

    def send_back(chunk):
        return pltpu.make_async_remote_copy(
            src_ref=returned.at[rows_of(chunk)],
            dst_ref=received.at[rows_of(chunk)],
            send_sem=back_out_sem.at[chunk],
            recv_sem=back_in_sem.at[chunk],
            device_id={"layer": preceding},
            device_id_type=MESH,
        )

    def one_back(index, gain_sum):
        chunk = chunks - 1 - index
        rows = rows_of(chunk)
        pltpu.make_async_copy(
            received.at[rows], received.at[rows], back_in_sem.at[chunk]
        ).wait()
        d_context = dot_nt(received[rows, :].astype(BF16), w_out[...]).astype(BF16)
        d_queries = []
        for head in range(HEADS):
            first = head * head_dim
            value = proj[1, :, 2 * width + first : 2 * width + first + head_dim]
            key = proj[1, :, width + first : width + first + head_dim]
            query = proj[1, rows, first : first + head_dim]
            prob = probs[1, head, rows, :]
            d_mixed = d_context[:, first : first + head_dim]
            d_prob = dot_nt(d_mixed, value)
            wide = prob.astype(F32)
            inner = jnp.sum(d_prob * wide, axis=-1, keepdims=True)
            d_score = (wide * (d_prob - inner) * scale).astype(BF16)
            d_queries.append(dot(d_score, key).astype(BF16))
            d_kv[:, first : first + head_dim] += dot_tn(d_score, query)
            d_kv[:, width + first : width + first + head_dim] += dot_tn(prob, d_mixed)
        d_proj = jnp.concatenate(d_queries + [d_kv[rows, :].astype(BF16)], axis=1)
        d_normed = dot_nt(d_proj, w_qkv[...])
        stream = ins[latest, rows, :]
        square = jnp.sum(stream * stream, axis=-1, keepdims=True) * (1.0 / width)
        root = lax.rsqrt(square + norm_eps)
        unit = stream * root
        gain_sum = gain_sum + jnp.sum(d_normed * unit, axis=0, keepdims=True)
        d_unit = d_normed * gain[...]
        slope = jnp.sum(d_unit * unit, axis=-1, keepdims=True) * (1.0 / width)
        returned[rows, :] = received[rows, :] + root * (d_unit - unit * slope)

        @pl.when(within > 0)
        def _():
            send_back(chunk).start()

        return gain_sum

    gain_sum = lax.fori_loop(0, chunks, one_back, jnp.zeros((1, width), F32))
    gain_parts[replica] = gain_sum

    def send_gain(offset):
        return pltpu.make_async_remote_copy(
            src_ref=gain_parts.at[replica],
            dst_ref=gain_parts.at[replica],
            send_sem=gain_out_sem.at[offset],
            recv_sem=gain_in_sem.at[replica],
            device_id={"dp": lax.rem(replica + offset, copies)},
            device_id_type=MESH,
        )

    for offset in range(1, copies):
        send_gain(offset).start()
    write_adjoints = pltpu.make_async_copy(returned, adjoints.at[0], final_sem.at[1])
    write_adjoints.start()

    @pl.when(gives_guess)
    def _():
        for chunk in range(chunks):
            send_guess(chunk, 1, following).wait_send()
            send_guess(chunk, 0, far_on).wait_send()

    @pl.when(gives_adjoint_guess)
    def _():
        for chunk in range(chunks):
            send_adjoint_guess(chunk).wait_send()

    @pl.when(within > 0)
    def _():
        for chunk in range(chunks):
            send_back(chunk).wait_send()

    def finish(task, carry):
        place = task // chunks
        chunk = task % chunks

        @pl.when(relays_fine(place))
        def _():
            send_next(place, chunk, place).wait_send()

        @pl.when(relays_first(place) | relays_second(place))
        def _():
            send_far(place, chunk, 2).wait_send()
            send_next(place, chunk, 3).wait_send()

        return carry

    lax.fori_loop(0, PASSES * chunks, finish, 0)

    for offset in range(1, copies):
        sender = lax.rem(replica + offset, copies)
        pltpu.make_async_copy(
            gain_parts.at[sender], gain_parts.at[sender], gain_in_sem.at[sender]
        ).wait()
        send_gain(offset).wait_send()
    grads[...] = jnp.sum(gain_parts[...], axis=0)
    write_states.wait()
    write_adjoints.wait()


def solution(mesh):
    depth = mesh.shape["layer"]
    copies = mesh.shape["dp"]

    def on_device(embedded, guess, qkv_weight, out_weight, norm_gain, cotangent, adjoint_guess):
        tokens, width = embedded.shape
        chunks = SEQ // ROWS
        anywhere = pl.BlockSpec(memory_space=pl.ANY)
        vector = pl.BlockSpec(memory_space=pltpu.VMEM)
        return pl.pallas_call(
            functools.partial(kernel, depth, copies),
            out_shape=(
                jax.ShapeDtypeStruct((1, tokens, width), F32),
                jax.ShapeDtypeStruct((1, tokens, width), F32),
                jax.ShapeDtypeStruct((1, width), F32),
            ),
            in_specs=[anywhere] * 4 + [vector] + [anywhere] * 2,
            out_specs=(anywhere, anywhere, vector),
            scratch_shapes=[
                pltpu.VMEM((width, 3 * width), BF16),
                pltpu.VMEM((width, width), BF16),
                pltpu.VMEM((PASSES, SEQ, width), F32),
                pltpu.VMEM((PASSES, SEQ, width), F32),
                pltpu.VMEM((SEQ, width), F32),
                pltpu.VMEM((2, SEQ, 3 * width), BF16),
                pltpu.VMEM((2, HEADS, SEQ, SEQ), BF16),
                pltpu.VMEM((ROWS, width), BF16),
                pltpu.VMEM((SEQ, width), F32),
                pltpu.VMEM((SEQ, width), F32),
                pltpu.VMEM((SEQ, 2 * width), F32),
                pltpu.VMEM((copies, 1, width), F32),
                pltpu.SemaphoreType.DMA((2,)),
                pltpu.SemaphoreType.DMA((PASSES, chunks)),
                pltpu.SemaphoreType.DMA((PASSES, chunks)),
                pltpu.SemaphoreType.DMA((PASSES, chunks)),
                pltpu.SemaphoreType.DMA((2, chunks)),
                pltpu.SemaphoreType.DMA((chunks,)),
                pltpu.SemaphoreType.DMA((chunks,)),
                pltpu.SemaphoreType.DMA((copies,)),
                pltpu.SemaphoreType.DMA((copies,)),
                pltpu.SemaphoreType.DMA((2,)),
            ],
            compiler_params=pltpu.CompilerParams(
                collective_id=0, has_side_effects=True, vmem_limit_bytes=48 * 2**20
            ),
        )(embedded, guess, qkv_weight, out_weight, norm_gain, cotangent, adjoint_guess)

    return jax.shard_map(
        on_device,
        mesh=mesh,
        in_specs=(
            P("dp", None),
            P("layer", "dp", None),
            P("layer", None, None),
            P("layer", None, None),
            P("layer", None),
            P("dp", None),
            P("layer", "dp", None),
        ),
        out_specs=(P("layer", "dp", None), P("layer", "dp", None), P("layer", None)),
        check_vma=False,
    )
```

```python
import functools

import jax
import jax.numpy as jnp
from jax import lax
from jax.experimental import pallas as pl
from jax.experimental.pallas import tpu as pltpu
from jax.sharding import PartitionSpec as P

HEADS = 8
SEQ = 128
ROWS = 32
PARTS = 4
PASSES = 6

coarse_ratio = 4.0
norm_eps = 1e-06

F32 = jnp.float32
BF16 = jnp.bfloat16
MESH = pl.DeviceIdType.MESH


def dot(a, b):
    return jnp.dot(a, b, preferred_element_type=F32)


def dot_nt(a, b):
    return lax.dot_general(a, b, (((1,), (1,)), ((), ())), preferred_element_type=F32)


def dot_tn(a, b):
    return lax.dot_general(a, b, (((0,), (0,)), ((), ())), preferred_element_type=F32)


def kernel(
    depth,
    copies,
    embedded,
    guess,
    qkv_weight,
    out_weight,
    norm_gain,
    cotangent,
    adjoint_guess,
    states,
    adjoints,
    grads,
    w_qkv,
    w_out,
    w_qkv_t,
    w_out_t,
    gain,
    ins,
    outs,
    base,
    proj,
    probs,
    received,
    returned,
    staged,
    gain_parts,
    weight_sem,
    load_sem,
    in_sem,
    out_sem,
    far_sem,
    guess_sem,
    back_in_sem,
    back_out_sem,
    gain_in_sem,
    gain_out_sem,
    final_sem,
):
    width = gain.shape[-1]
    head_dim = width // HEADS
    part_width = width // PARTS
    chunks = SEQ // ROWS
    groups = depth // 4
    me = lax.axis_index("layer")
    replica = lax.axis_index("dp")
    group = me // 4
    within = me % 4
    following = lax.rem(me + 1, depth)
    preceding = lax.rem(me + depth - 1, depth)
    far_on = lax.rem(me + 4, depth)
    far_back = lax.rem(me + depth - 4, depth)

    barrier = pltpu.get_barrier_semaphore()
    for neighbour in (following, preceding):
        pl.semaphore_signal(
            barrier, inc=1, device_id={"layer": neighbour}, device_id_type=MESH
        )
    for offset in range(1, copies):
        pl.semaphore_signal(
            barrier,
            inc=1,
            device_id={"dp": lax.rem(replica + offset, copies)},
            device_id_type=MESH,
        )

    @pl.when(within == 3)
    def _():
        for neighbour in (far_on, far_back):
            pl.semaphore_signal(
                barrier, inc=1, device_id={"layer": neighbour}, device_id_type=MESH
            )

    def rows_of(chunk):
        return pl.ds(pl.multiple_of(chunk * ROWS, ROWS), ROWS)

    def cols_of(part):
        return pl.ds(part * part_width, part_width)

    load_gain = pltpu.make_async_copy(norm_gain, gain, load_sem.at[0])
    load_gain.start()
    load_guess = pltpu.make_async_copy(guess.at[0], staged, load_sem.at[1])
    gives_guess = (within == 3) & (group < groups - 1)
    gives_adjoint_guess = (within == 0) & (group > 0)

    @pl.when(gives_guess)
    def _():
        load_guess.start()

    def embed_copy(chunk, part):
        return pltpu.make_async_copy(
            embedded.at[rows_of(chunk), cols_of(part)],
            ins.at[1, part, rows_of(chunk)],
            in_sem.at[1, chunk, part],
        )

    load_cotangent = pltpu.make_async_copy(cotangent, received, back_in_sem.at[0])

    @pl.when(me == 0)
    def _():
        for chunk in range(chunks):
            for part in range(PARTS):
                embed_copy(chunk, part).start()

    def load_qkv(part):
        return pltpu.make_async_copy(
            qkv_weight.at[0, cols_of(part)], w_qkv.at[cols_of(part)], weight_sem.at[part]
        )

    load_out = pltpu.make_async_copy(out_weight.at[0], w_out, weight_sem.at[PARTS])
    for part in range(PARTS):
        load_qkv(part).start()
    load_out.start()

    @pl.when(me == depth - 1)
    def _():
        load_cotangent.start()

    proj[...] = jnp.zeros_like(proj)

    @pl.when(me > 0)
    def _():
        pl.semaphore_wait(barrier, copies + 1 + 2 * (within // 3))

    def send_guess(chunk, part, place, target):
        return pltpu.make_async_remote_copy(
            src_ref=staged.at[rows_of(chunk), cols_of(part)],
            dst_ref=ins.at[place, part, rows_of(chunk)],
            send_sem=guess_sem.at[place],
            recv_sem=in_sem.at[place, chunk, part],
            device_id={"layer": target},
            device_id_type=MESH,
        )

    send_adjoint_guess = pltpu.make_async_remote_copy(
        src_ref=adjoint_guess.at[0],
        dst_ref=received,
        send_sem=back_out_sem.at[0],
        recv_sem=back_in_sem.at[0],
        device_id={"layer": preceding},
        device_id_type=MESH,
    )

    @pl.when(gives_guess)
    def _():
        load_guess.wait()

        @pl.loop(0, chunks)
        def _(chunk):
            for part in range(PARTS):
                send_guess(chunk, part, 1, following).start()

        @pl.loop(0, chunks)
        def _(chunk):
            for part in range(PARTS):
                send_guess(chunk, part, 0, far_on).start()

    @pl.when(gives_adjoint_guess)
    def _():
        send_adjoint_guess.start()

    load_gain.wait()

    def is_active(place):
        needed = jnp.where(place == 0, 1, place // 2)
        return ((within == 3) | (place % 2 == 1)) & (group >= needed)

    def relays_fine(place):
        return is_active(place) & (within < 3)

    def relays_first(place):
        right = ((group == 0) & (place == 1)) | ((group >= 1) & (place == 2))
        return (within == 3) & (group < groups - 1) & right

    def relays_second(place):
        right = ((group == 1) & (place == 3)) | ((group >= 2) & (place == 4))
        return (within == 3) & (group < groups - 1) & right

    first_place = jnp.where((within == 3) & (group >= 1), 0, 1)

    def send_main(place, chunk, part):
        second = relays_second(place)
        swapped = second & (group == groups - 2)
        fine = within < 3
        slot = jnp.where(second, 4, 2)
        target = jnp.where(fine | swapped, following, far_on)
        to_place = jnp.where(fine, place, jnp.where(swapped, slot + 1, slot))
        return pltpu.make_async_remote_copy(
            src_ref=outs.at[place, part, rows_of(chunk)],
            dst_ref=ins.at[to_place, part, rows_of(chunk)],
            send_sem=out_sem.at[place],
            recv_sem=in_sem.at[to_place, chunk, part],
            device_id={"layer": target},
            device_id_type=MESH,
        )

    def send_other(place, chunk, part):
        second = relays_second(place)
        swapped = second & (group == groups - 2)
        slot = jnp.where(second, 4, 2)
        target = jnp.where(swapped, far_on, following)
        to_place = jnp.where(swapped, slot, slot + 1)
        return pltpu.make_async_remote_copy(
            src_ref=outs.at[place, part, rows_of(chunk)],
            dst_ref=ins.at[to_place, part, rows_of(chunk)],
            send_sem=far_sem.at[place],
            recv_sem=in_sem.at[to_place, chunk, part],
            device_id={"layer": target},
            device_id_type=MESH,
        )

    causal_cols = lax.broadcasted_iota(jnp.int32, (ROWS, SEQ), 1)
    causal_rows = lax.broadcasted_iota(jnp.int32, (ROWS, SEQ), 0)
    scale = head_dim**-0.5

    def mix_parts(places, chunk, parities):
        rows = rows_of(chunk)
        total = None
        for part in range(PARTS):
            cols = cols_of(part)
            for place in places:
                pltpu.make_async_copy(
                    ins.at[place, part, rows],
                    ins.at[place, part, rows],
                    in_sem.at[place, chunk, part],
                ).wait()
            stream = jnp.concatenate([ins[place, part, rows, :] for place in places], axis=0)
            square = jnp.sum(stream * stream, axis=-1, keepdims=True)
            product = dot((stream * gain[:, cols]).astype(BF16), w_qkv[cols, :])
            if total is None:
                total, squares = product, square
            else:
                total, squares = total + product, squares + square
        root = lax.rsqrt(squares * (1.0 / width) + norm_eps)
        projected = (total * root).astype(BF16)
        for index, place in enumerate(places):
            proj[parities[index], rows, :] = projected[index * ROWS : (index + 1) * ROWS]
        causal = causal_rows + chunk * ROWS >= causal_cols
        work = [(index, place, head) for index, place in enumerate(places) for head in range(HEADS)]
        scores = []
        for index, place, head in work:
            first_col = head * head_dim
            query = projected[index * ROWS : (index + 1) * ROWS, first_col : first_col + head_dim]
            key = proj[parities[index], :, width + first_col : width + first_col + head_dim]
            scores.append(jnp.where(causal, dot_nt(query, key) * scale, -1e30))
        exps = [jnp.exp(s - jnp.max(s, axis=-1, keepdims=True)) for s in scores]
        inverses = [1.0 / jnp.sum(e, axis=-1, keepdims=True) for e in exps]
        mixed = []
        for (index, place, head), e, inverse in zip(work, exps, inverses):
            first_col = head * head_dim
            value = proj[parities[index], :, 2 * width + first_col : 2 * width + first_col + head_dim]
            mixed.append((dot(e.astype(BF16), value) * inverse).astype(BF16))
        contexts = [
            jnp.concatenate(mixed[index * HEADS : (index + 1) * HEADS], axis=1)
            for index in range(len(places))
        ]
        return jnp.concatenate(contexts, axis=0), exps, inverses

    def keep_probs(exps, inverses, chunk):
        for head in range(HEADS):
            probs[head, rows_of(chunk), :] = (exps[head] * inverses[head]).astype(BF16)

    def send_others(place, chunk):
        @pl.when(relays_first(place) | relays_second(place))
        def _():
            for part in range(PARTS):
                send_other(place, chunk, part).start()

    def one_pass(place, chunk):
        rows = rows_of(chunk)
        first = (chunk == 0) & (place == first_place)

        @pl.when(first)
        def _():
            for part in range(PARTS):
                load_qkv(part).wait()
            load_out.wait()

        context, exps, inverses = mix_parts((place,), chunk, (place % 2,))

        @pl.when((within < 3) | (place < 5))
        def _():
            odd = place % 2 == 1
            ratio = jnp.where(odd, 1.0, coarse_ratio)
            mix = dot(context, w_out[...])
            for part in range(PARTS):
                cols = slice(part * part_width, (part + 1) * part_width)
                step = ins[place, part, rows, :] + ratio * mix[:, cols]
                outs[place, part, rows, :] = step
                base[part, rows, :] = -step

            @pl.when(first & (me == 0))
            def _():
                pl.semaphore_wait(barrier, copies + 1)

            @pl.when(relays_fine(place) | relays_first(place) | relays_second(place))
            def _():
                for part in range(PARTS):
                    send_main(place, chunk, part).start()

            send_others(place, chunk)

        keep_probs(exps, inverses, chunk)

        @pl.when((chunk == chunks - 1) & (place == first_place))
        def _():
            w_out_t[...] = w_out[...].T

            @pl.loop(0, 3 * PARTS)
            def _(block):
                cols = pl.ds(pl.multiple_of(block * part_width, part_width), part_width)
                w_qkv_t[cols, :] = w_qkv[:, cols].T

    def two_passes(place, chunk):
        rows = rows_of(chunk)
        coarse = place + 1
        context, _, _ = mix_parts((place, coarse), chunk, (1, 0))
        mix = dot(context, w_out[...])
        for part in range(PARTS):
            cols = slice(part * part_width, (part + 1) * part_width)
            end = base[part, rows, :] + (ins[place, part, rows, :] + mix[:ROWS, cols])
            step = ins[coarse, part, rows, :] + coarse_ratio * mix[ROWS:, cols]
            outs[coarse, part, rows, :] = end + step
            base[part, rows, :] = -step

        @pl.when(relays_first(coarse) | relays_second(coarse))
        def _():
            for part in range(PARTS):
                send_main(coarse, chunk, part).start()

        send_others(coarse, chunk)

    def one_task(task, carry):
        turn = task // chunks
        chunk = task % chunks
        place = turn + turn // 2 + turn // 3
        paired = (
            (within == 3)
            & (place % 2 == 1)
            & (place <= 3)
            & (group >= place // 2 + 1)
        )

        @pl.when(is_active(place) & jnp.logical_not(paired))
        def _():
            one_pass(place, chunk)

        @pl.when(paired)
        def _():
            two_passes(place, chunk)

        return carry

    lax.fori_loop(0, 4 * chunks, one_task, 0)

    latest = 1 + 2 * jnp.minimum(group, 2)
    final = latest - jnp.where((within == 3) & (group >= 2), 1, 0)

    def write_states(part):
        return pltpu.make_async_copy(
            outs.at[final, part], states.at[0, :, cols_of(part)], final_sem.at[part]
        )

    for part in range(PARTS):
        write_states(part).start()

    send_back = pltpu.make_async_remote_copy(
        src_ref=returned,
        dst_ref=received,
        send_sem=back_out_sem.at[0],
        recv_sem=back_in_sem.at[0],
        device_id={"layer": preceding},
        device_id_type=MESH,
    )

    pltpu.make_async_copy(received, received, back_in_sem.at[0]).wait()
    d_context = dot(received[...].astype(BF16), w_out_t[...]).astype(BF16)
    heads = [slice(head * head_dim, (head + 1) * head_dim) for head in range(HEADS)]

    def kind(number, head):
        return slice(number * width + head * head_dim, number * width + (head + 1) * head_dim)

    d_probs = [dot_nt(d_context[:, heads[h]], proj[1, :, kind(2, h)]) for h in range(HEADS)]
    wides = [probs[h].astype(F32) for h in range(HEADS)]
    weighted = [d * p for d, p in zip(d_probs, wides)]
    inners = [jnp.sum(w, axis=-1, keepdims=True) for w in weighted]
    d_scores = [
        ((w - p * n) * scale).astype(BF16) for w, p, n in zip(weighted, wides, inners)
    ]
    d_query = [dot(d_scores[h], proj[1, :, kind(1, h)]).astype(BF16) for h in range(HEADS)]
    d_key = [dot_tn(d_scores[h], proj[1, :, kind(0, h)]).astype(BF16) for h in range(HEADS)]
    d_value = [dot_tn(probs[h], d_context[:, heads[h]]).astype(BF16) for h in range(HEADS)]
    d_normed = dot(jnp.concatenate(d_query + d_key + d_value, axis=1), w_qkv_t[...])
    stream = jnp.concatenate([ins[latest, part] for part in range(PARTS)], axis=1)
    square = jnp.sum(stream * stream, axis=-1, keepdims=True) * (1.0 / width)
    root = lax.rsqrt(square + norm_eps)
    unit = stream * root
    d_unit = d_normed * gain[...]
    slope = jnp.sum(d_unit * unit, axis=-1, keepdims=True) * (1.0 / width)
    returned[...] = received[...] + root * (d_unit - unit * slope)

    @pl.when(within > 0)
    def _():
        send_back.start()

    gain_parts[replica] = jnp.sum(d_normed * unit, axis=0, keepdims=True)

    def send_gain(offset):
        return pltpu.make_async_remote_copy(
            src_ref=gain_parts.at[replica],
            dst_ref=gain_parts.at[replica],
            send_sem=gain_out_sem.at[offset],
            recv_sem=gain_in_sem.at[replica],
            device_id={"dp": lax.rem(replica + offset, copies)},
            device_id_type=MESH,
        )

    for offset in range(1, copies):
        send_gain(offset).start()
    write_adjoints = pltpu.make_async_copy(returned, adjoints.at[0], final_sem.at[PARTS])
    write_adjoints.start()

    @pl.when(gives_guess)
    def _():
        for place in range(2):
            pltpu.make_async_copy(staged, staged, guess_sem.at[place]).wait()

    @pl.when(gives_adjoint_guess)
    def _():
        send_adjoint_guess.wait_send()

    @pl.when(within > 0)
    def _():
        send_back.wait_send()

    @pl.loop(0, PASSES)
    def _(place):
        sent = outs.at[place]

        @pl.when(relays_fine(place) | relays_first(place) | relays_second(place))
        def _():
            pltpu.make_async_copy(sent, sent, out_sem.at[place]).wait()

        @pl.when(relays_first(place) | relays_second(place))
        def _():
            pltpu.make_async_copy(sent, sent, far_sem.at[place]).wait()

    for offset in range(1, copies):
        sender = lax.rem(replica + offset, copies)
        pltpu.make_async_copy(
            gain_parts.at[sender], gain_parts.at[sender], gain_in_sem.at[sender]
        ).wait()
        send_gain(offset).wait_send()
    grads[...] = jnp.sum(gain_parts[...], axis=0)
    for part in range(PARTS):
        write_states(part).wait()
    write_adjoints.wait()


def write_out(states_in, adjoints_in, grads_in, states, adjoints, grads):
    states[...] = states_in[...]
    adjoints[...] = adjoints_in[...]
    grads[...] = grads_in[...]


def solution(mesh):
    depth = mesh.shape["layer"]
    copies = mesh.shape["dp"]

    def on_device(embedded, guess, qkv_weight, out_weight, norm_gain, cotangent, adjoint_guess):
        tokens, width = embedded.shape
        chunks = SEQ // ROWS
        anywhere = pl.BlockSpec(memory_space=pl.ANY)
        vector = pl.BlockSpec(memory_space=pltpu.VMEM)
        results = pl.pallas_call(
            functools.partial(kernel, depth, copies),
            out_shape=(
                jax.ShapeDtypeStruct((1, tokens, width), F32),
                jax.ShapeDtypeStruct((1, tokens, width), F32),
                jax.ShapeDtypeStruct((1, width), F32),
            ),
            in_specs=[anywhere] * 7,
            out_specs=(anywhere, anywhere, vector),
            scratch_shapes=[
                pltpu.VMEM((width, 3 * width), BF16),
                pltpu.VMEM((width, width), BF16),
                pltpu.VMEM((3 * width, width), BF16),
                pltpu.VMEM((width, width), BF16),
                pltpu.VMEM((1, width), F32),
                pltpu.VMEM((PASSES, PARTS, SEQ, width // PARTS), F32),
                pltpu.VMEM((PASSES, PARTS, SEQ, width // PARTS), F32),
                pltpu.VMEM((PARTS, SEQ, width // PARTS), F32),
                pltpu.VMEM((2, SEQ, 3 * width), BF16),
                pltpu.VMEM((HEADS, SEQ, SEQ), BF16),
                pltpu.VMEM((SEQ, width), F32),
                pltpu.VMEM((SEQ, width), F32),
                pltpu.VMEM((SEQ, width), F32),
                pltpu.VMEM((copies, 1, width), F32),
                pltpu.SemaphoreType.DMA((PARTS + 1,)),
                pltpu.SemaphoreType.DMA((2,)),
                pltpu.SemaphoreType.DMA((PASSES, chunks, PARTS)),
                pltpu.SemaphoreType.DMA((PASSES,)),
                pltpu.SemaphoreType.DMA((PASSES,)),
                pltpu.SemaphoreType.DMA((2,)),
                pltpu.SemaphoreType.DMA((1,)),
                pltpu.SemaphoreType.DMA((1,)),
                pltpu.SemaphoreType.DMA((copies,)),
                pltpu.SemaphoreType.DMA((copies,)),
                pltpu.SemaphoreType.DMA((PARTS + 1,)),
            ],
            compiler_params=pltpu.CompilerParams(
                collective_id=0, has_side_effects=True, vmem_limit_bytes=60 * 2**20
            ),
        )(embedded, guess, qkv_weight, out_weight, norm_gain, cotangent, adjoint_guess)
        return pl.pallas_call(
            write_out,
            out_shape=tuple(jax.ShapeDtypeStruct(r.shape, r.dtype) for r in results),
            in_specs=[vector] * 3,
            out_specs=(vector,) * 3,
        )(*results)

    return jax.shard_map(
        on_device,
        mesh=mesh,
        in_specs=(
            P("dp", None),
            P("layer", "dp", None),
            P("layer", None, None),
            P("layer", None, None),
            P("layer", None),
            P("dp", None),
            P("layer", "dp", None),
        ),
        out_specs=(P("layer", "dp", None), P("layer", "dp", None), P("layer", None)),
        check_vma=False,
    )
```

```python
import functools

import jax
import jax.numpy as jnp
from jax import lax
from jax.experimental import pallas as pl
from jax.experimental.pallas import tpu as pltpu
from jax.sharding import PartitionSpec as P

HEADS = 8
SEQ = 128
ROWS = 32
PARTS = 8
PASSES = 6
HALVES = 2
BACK_PARTS = 4
TURNS = 4

coarse_ratio = 4.0
norm_eps = 1e-06

F32 = jnp.float32
BF16 = jnp.bfloat16
MESH = pl.DeviceIdType.MESH


def dot(a, b):
    return jnp.dot(a, b, preferred_element_type=F32)


def dot_nt(a, b):
    return lax.dot_general(a, b, (((1,), (1,)), ((), ())), preferred_element_type=F32)


def dot_tn(a, b):
    return lax.dot_general(a, b, (((0,), (0,)), ((), ())), preferred_element_type=F32)


def kernel(
    depth,
    copies,
    embedded,
    guess,
    qkv_weight,
    out_weight,
    norm_gain,
    cotangent,
    adjoint_guess,
    states,
    adjoints,
    grads,
    w_qkv,
    w_out,
    w_qkv_t,
    w_out_t,
    gain,
    ins,
    outs,
    base,
    proj,
    probs,
    received,
    returned,
    d_context_ref,
    staged,
    gain_parts,
    weight_sem,
    load_sem,
    in_sem,
    out_sem,
    far_sem,
    guess_sem,
    back_in_sem,
    back_out_sem,
    gain_in_sem,
    gain_out_sem,
    final_sem,
):
    width = gain.shape[-1]
    head_dim = width // HEADS
    part_width = width // PARTS
    back_width = width // BACK_PARTS
    chunks = SEQ // ROWS
    groups = depth // 4
    me = lax.axis_index("layer")
    replica = lax.axis_index("dp")
    group = me // 4
    within = me % 4
    following = lax.rem(me + 1, depth)
    preceding = lax.rem(me + depth - 1, depth)
    far_on = lax.rem(me + 4, depth)
    far_back = lax.rem(me + depth - 4, depth)

    def rows_of(chunk):
        return pl.ds(pl.multiple_of(chunk * ROWS, ROWS), ROWS)

    def cols_of(part):
        return pl.ds(part * part_width, part_width)

    def load_qkv(part):
        return pltpu.make_async_copy(
            qkv_weight.at[0, cols_of(part)], w_qkv.at[cols_of(part)], weight_sem.at[part]
        )

    load_out = pltpu.make_async_copy(out_weight.at[0], w_out, weight_sem.at[PARTS])
    load_gain = pltpu.make_async_copy(norm_gain, gain, load_sem.at[0])
    load_guess = pltpu.make_async_copy(guess.at[0], staged, load_sem.at[1])
    gives_guess = (within == 3) & (group < groups - 1)
    gives_adjoint_guess = (within == 0) & (group > 0)
    for part in range(PARTS):
        load_qkv(part).start()
    load_out.start()
    load_gain.start()

    @pl.when(gives_guess)
    def _():
        load_guess.start()

    barrier = pltpu.get_barrier_semaphore()
    for neighbour in (following, preceding):
        pl.semaphore_signal(
            barrier, inc=1, device_id={"layer": neighbour}, device_id_type=MESH
        )
    for offset in range(1, copies):
        pl.semaphore_signal(
            barrier,
            inc=1,
            device_id={"dp": lax.rem(replica + offset, copies)},
            device_id_type=MESH,
        )

    @pl.when(within == 3)
    def _():
        for neighbour in (far_on, far_back):
            pl.semaphore_signal(
                barrier, inc=1, device_id={"layer": neighbour}, device_id_type=MESH
            )

    @pl.when(me == 0)
    def _():
        @pl.loop(0, chunks)
        def _(chunk):
            for part in range(PARTS):
                pltpu.make_async_copy(
                    embedded.at[rows_of(chunk), cols_of(part)],
                    ins.at[1, part, rows_of(chunk)],
                    in_sem.at[1, chunk, part],
                ).start()

    @pl.when(me == depth - 1)
    def _():
        for part in range(BACK_PARTS):
            pltpu.make_async_copy(
                cotangent.at[:, pl.ds(part * back_width, back_width)],
                received.at[part],
                back_in_sem.at[part],
            ).start()

    proj[...] = jnp.zeros_like(proj)

    @pl.when(me > 0)
    def _():
        pl.semaphore_wait(barrier, copies + 1 + 2 * (within // 3))

    def send_guess(chunk, part, place, target):
        return pltpu.make_async_remote_copy(
            src_ref=staged.at[rows_of(chunk), cols_of(part)],
            dst_ref=ins.at[place, part, rows_of(chunk)],
            send_sem=guess_sem.at[place],
            recv_sem=in_sem.at[place, chunk, part],
            device_id={"layer": target},
            device_id_type=MESH,
        )

    def send_adjoint_guess(part):
        return pltpu.make_async_remote_copy(
            src_ref=adjoint_guess.at[0, :, pl.ds(part * back_width, back_width)],
            dst_ref=received.at[part],
            send_sem=back_out_sem.at[0],
            recv_sem=back_in_sem.at[part],
            device_id={"layer": preceding},
            device_id_type=MESH,
        )

    @pl.when(gives_guess)
    def _():
        load_guess.wait()

        @pl.loop(0, chunks)
        def _(chunk):
            for part in range(PARTS):
                send_guess(chunk, part, 1, following).start()

        @pl.loop(0, chunks)
        def _(chunk):
            for part in range(PARTS):
                send_guess(chunk, part, 0, far_on).start()

    @pl.when(gives_adjoint_guess)
    def _():
        for part in range(BACK_PARTS):
            send_adjoint_guess(part).start()

    load_gain.wait()

    def is_active(place):
        needed = jnp.where(place == 0, 1, place // 2)
        return ((within == 3) | (place % 2 == 1)) & (group >= needed)

    def relays_fine(place):
        return is_active(place) & (within < 3)

    def relays_first(place):
        right = ((group == 0) & (place == 1)) | ((group >= 1) & (place == 2))
        return (within == 3) & (group < groups - 1) & right

    def relays_second(place):
        right = ((group == 1) & (place == 3)) | ((group >= 2) & (place == 4))
        return (within == 3) & (group < groups - 1) & right

    def send_main(place, chunk, part):
        second = relays_second(place)
        swapped = second & (group == groups - 2)
        fine = within < 3
        slot = jnp.where(second, 4, 2)
        target = jnp.where(fine | swapped, following, far_on)
        to_place = jnp.where(fine, place, jnp.where(swapped, slot + 1, slot))
        return pltpu.make_async_remote_copy(
            src_ref=outs.at[place, part, rows_of(chunk)],
            dst_ref=ins.at[to_place, part, rows_of(chunk)],
            send_sem=out_sem.at[place],
            recv_sem=in_sem.at[to_place, chunk, part],
            device_id={"layer": target},
            device_id_type=MESH,
        )

    def send_other(place, chunk, part):
        second = relays_second(place)
        swapped = second & (group == groups - 2)
        slot = jnp.where(second, 4, 2)
        target = jnp.where(swapped, far_on, following)
        to_place = jnp.where(swapped, slot, slot + 1)
        return pltpu.make_async_remote_copy(
            src_ref=outs.at[place, part, rows_of(chunk)],
            dst_ref=ins.at[to_place, part, rows_of(chunk)],
            send_sem=far_sem.at[place],
            recv_sem=in_sem.at[to_place, chunk, part],
            device_id={"layer": target},
            device_id_type=MESH,
        )

    half_cols = [
        slice(half * (width // HALVES), (half + 1) * (width // HALVES)) for half in range(HALVES)
    ]
    causal_cols = lax.broadcasted_iota(jnp.int32, (ROWS, SEQ), 1)
    causal_rows = lax.broadcasted_iota(jnp.int32, (ROWS, SEQ), 0)
    scale = head_dim**-0.5

    def mix_parts(streams):
        total = None
        for part in range(PARTS):
            cols = cols_of(part)
            for place, chunk, _ in streams:
                pltpu.make_async_copy(
                    ins.at[place, part, rows_of(chunk)],
                    ins.at[place, part, rows_of(chunk)],
                    in_sem.at[place, chunk, part],
                ).wait()
            stream = jnp.concatenate(
                [ins[place, part, rows_of(chunk), :] for place, chunk, _ in streams], axis=0
            )
            square = jnp.sum(stream * stream, axis=-1, keepdims=True)
            product = dot((stream * gain[:, cols]).astype(BF16), w_qkv[cols, :])
            if total is None:
                total, squares = product, square
            else:
                total, squares = total + product, squares + square
        root = lax.rsqrt(squares * (1.0 / width) + norm_eps)
        projected = (total * root).astype(BF16)
        pieces = [projected[i * ROWS : (i + 1) * ROWS] for i in range(len(streams))]
        for piece, (_, chunk, which) in zip(pieces, streams):
            proj[which, rows_of(chunk), :] = piece
        work = [
            (piece, chunk, which, head * head_dim)
            for piece, (_, chunk, which) in zip(pieces, streams)
            for head in range(HEADS)
        ]
        scores = []
        for piece, chunk, which, first_col in work:
            causal = causal_rows + chunk * ROWS >= causal_cols
            query = piece[:, first_col : first_col + head_dim]
            key = proj[which, :, width + first_col : width + first_col + head_dim]
            scores.append(jnp.where(causal, dot_nt(query, key) * scale, -1e30))
        exps = [jnp.exp(s - jnp.max(s, axis=-1, keepdims=True)) for s in scores]
        inverses = [1.0 / jnp.sum(e, axis=-1, keepdims=True) for e in exps]
        mixed = []
        for (_, _, which, first_col), e, inverse in zip(work, exps, inverses):
            value = proj[which, :, 2 * width + first_col : 2 * width + first_col + head_dim]
            mixed.append((dot(e.astype(BF16), value) * inverse).astype(BF16))
        contexts = [
            jnp.concatenate(mixed[i * HEADS : (i + 1) * HEADS], axis=1)
            for i in range(len(streams))
        ]
        return jnp.concatenate(contexts, axis=0), exps, inverses

    def keep_probs(exps, inverses, chunk):
        for head in range(HEADS):
            probs[head, rows_of(chunk), :] = (exps[head] * inverses[head]).astype(BF16)

    def send_others(place, chunk):
        @pl.when(relays_first(place) | relays_second(place))
        def _():
            for part in range(PARTS):
                send_other(place, chunk, part).start()

    def one_pass(place, chunk):
        rows = rows_of(chunk)
        context, exps, inverses = mix_parts(((place, chunk, place % 2),))

        @pl.when(place == 0)
        def _():
            mix = dot(context, w_out[...])
            for part in range(PARTS):
                cols = slice(part * part_width, (part + 1) * part_width)
                base[part, rows, :] = -(ins[place, part, rows, :] + coarse_ratio * mix[:, cols])

        @pl.when((within < 3) | (group == 0))
        def _():
            halves = [dot(context, w_out[:, cols]) for cols in half_cols]

            @pl.when((me == 0) & (chunk == 0))
            def _():
                pl.semaphore_wait(barrier, copies + 1)

            for half, mix in enumerate(halves):
                for step in range(PARTS // HALVES):
                    part = half * (PARTS // HALVES) + step
                    cols = slice(step * part_width, (step + 1) * part_width)
                    outs[place, part, rows, :] = ins[place, part, rows, :] + mix[:, cols]
                for step in range(PARTS // HALVES):
                    send_main(place, chunk, half * (PARTS // HALVES) + step).start()
            send_others(place, chunk)

        keep_probs(exps, inverses, chunk)

    def transpose_weights():
        w_out_t[...] = w_out[...].T

        @pl.loop(0, 3 * TURNS)
        def _(block):
            turn_width = width // TURNS
            cols = pl.ds(pl.multiple_of(block * turn_width, turn_width), turn_width)
            w_qkv_t[cols, :] = w_qkv[:, cols].T

    def pull_known():
        for part in range(BACK_PARTS):
            pltpu.make_async_copy(received.at[part], received.at[part], back_in_sem.at[part]).wait()
        known = jnp.concatenate([received[part] for part in range(BACK_PARTS)], axis=1)
        d_context_ref[...] = dot(known.astype(BF16), w_out_t[...]).astype(BF16)

    def two_passes(place, chunk, paired):
        other_place = jnp.where(paired, place + 1, place)
        other_chunk = jnp.where(paired, chunk, chunk + 1)
        rows = rows_of(chunk)
        other_rows = rows_of(other_chunk)
        context, exps, inverses = mix_parts(
            ((place, chunk, 1), (other_place, other_chunk, jnp.where(paired, 0, 1)))
        )
        mix = dot(context, w_out[...])

        @pl.when(paired)
        def _():
            for part in range(PARTS):
                cols = slice(part * part_width, (part + 1) * part_width)
                end = base[part, rows, :] + (ins[place, part, rows, :] + mix[:ROWS, cols])
                step = ins[other_place, part, rows, :] + coarse_ratio * mix[ROWS:, cols]
                outs[other_place, part, rows, :] = end + step
                base[part, rows, :] = -step

        @pl.when(jnp.logical_not(paired))
        def _():
            for part in range(PARTS):
                cols = slice(part * part_width, (part + 1) * part_width)
                outs[place, part, rows, :] = ins[place, part, rows, :] + mix[:ROWS, cols]
                outs[place, part, other_rows, :] = (
                    ins[place, part, other_rows, :] + mix[ROWS:, cols]
                )
            for part in range(PARTS):
                send_main(place, chunk, part).start()

        @pl.when(relays_first(other_place) | relays_second(other_place))
        def _():
            for part in range(PARTS):
                send_main(other_place, other_chunk, part).start()

        @pl.when(jnp.logical_not(paired))
        def _():
            send_others(place, chunk)
            keep_probs(exps[:HEADS], inverses[:HEADS], chunk)
            keep_probs(exps[HEADS:], inverses[HEADS:], other_chunk)

        send_others(other_place, other_chunk)

    def one_task(task, carry):
        turn = task // chunks
        chunk = task % chunks
        place = turn + turn // 2 + turn // 3
        ends = within == 3
        paired = ends & (((group >= 1) & (place == 1)) | ((group >= 2) & (place == 3)))
        joined = ends & (group == 1) & (place == 3)
        early = ends & (group > 0)

        @pl.when((early & (task == 0)) | (jnp.logical_not(early) & (task == 2 * chunks)))
        def _():
            transpose_weights()

        @pl.when(ends & (group >= 2) & (task == 3 * chunks))
        def _():
            pull_known()

        @pl.when(is_active(place) & jnp.logical_not(paired | joined))
        def _():
            one_pass(place, chunk)

        @pl.when(paired | (joined & (chunk % 2 == 0)))
        def _():
            two_passes(place, chunk, paired)

        return carry

    for part in range(PARTS):
        load_qkv(part).wait()
    load_out.wait()
    lax.fori_loop(0, 4 * chunks, one_task, 0)

    latest = 1 + 2 * jnp.minimum(group, 2)
    final = latest - jnp.where((within == 3) & (group >= 2), 1, 0)

    def write_states(part):
        return pltpu.make_async_copy(
            outs.at[final, part], states.at[0, :, cols_of(part)], final_sem.at[part]
        )

    for part in range(PARTS):
        write_states(part).start()

    def send_back(part):
        return pltpu.make_async_remote_copy(
            src_ref=returned.at[part],
            dst_ref=received.at[part],
            send_sem=back_out_sem.at[0],
            recv_sem=back_in_sem.at[part],
            device_id={"layer": preceding},
            device_id_type=MESH,
        )

    @pl.when((within == 3) & (group < 2))
    def _():
        pull_known()

    @pl.when(within < 3)
    def _():
        total = None
        for part in range(BACK_PARTS):
            pltpu.make_async_copy(received.at[part], received.at[part], back_in_sem.at[part]).wait()
            cols = slice(part * back_width, (part + 1) * back_width)
            product = dot(received[part].astype(BF16), w_out_t[cols, :])
            total = product if total is None else total + product
        d_context_ref[...] = total.astype(BF16)

    d_context = d_context_ref[...]
    heads = [slice(head * head_dim, (head + 1) * head_dim) for head in range(HEADS)]

    def kind(number, head):
        return slice(number * width + head * head_dim, number * width + (head + 1) * head_dim)

    d_probs = [dot_nt(d_context[:, heads[h]], proj[1, :, kind(2, h)]) for h in range(HEADS)]
    wides = [probs[h].astype(F32) for h in range(HEADS)]
    weighted = [d * p for d, p in zip(d_probs, wides)]
    inners = [jnp.sum(w, axis=-1, keepdims=True) for w in weighted]
    d_scores = [
        ((w - p * n) * scale).astype(BF16) for w, p, n in zip(weighted, wides, inners)
    ]
    d_query = [dot(d_scores[h], proj[1, :, kind(1, h)]).astype(BF16) for h in range(HEADS)]
    d_key = [dot_tn(d_scores[h], proj[1, :, kind(0, h)]).astype(BF16) for h in range(HEADS)]
    d_value = [dot_tn(probs[h], d_context[:, heads[h]]).astype(BF16) for h in range(HEADS)]
    d_normed = dot(jnp.concatenate(d_query + d_key + d_value, axis=1), w_qkv_t[...])
    stream = jnp.concatenate([ins[latest, part] for part in range(PARTS)], axis=1)
    square = jnp.sum(stream * stream, axis=-1, keepdims=True) * (1.0 / width)
    root = lax.rsqrt(square + norm_eps)
    unit = stream * root
    d_unit = d_normed * gain[...]
    slope = jnp.sum(d_unit * unit, axis=-1, keepdims=True) * (1.0 / width)
    pulled = root * (d_unit - unit * slope)
    for part in range(BACK_PARTS):
        cols = slice(part * back_width, (part + 1) * back_width)
        returned[part] = received[part] + pulled[:, cols]

    @pl.when(within > 0)
    def _():
        for part in range(BACK_PARTS):
            send_back(part).start()

    gain_parts[replica] = jnp.sum(d_normed * unit, axis=0, keepdims=True)

    def send_gain(offset):
        return pltpu.make_async_remote_copy(
            src_ref=gain_parts.at[replica],
            dst_ref=gain_parts.at[replica],
            send_sem=gain_out_sem.at[offset],
            recv_sem=gain_in_sem.at[replica],
            device_id={"dp": lax.rem(replica + offset, copies)},
            device_id_type=MESH,
        )

    for offset in range(1, copies):
        send_gain(offset).start()

    def write_adjoints(part):
        return pltpu.make_async_copy(
            returned.at[part],
            adjoints.at[0, :, pl.ds(part * back_width, back_width)],
            final_sem.at[PARTS + part],
        )

    for part in range(BACK_PARTS):
        write_adjoints(part).start()

    @pl.when(gives_guess)
    def _():
        for place in range(2):
            pltpu.make_async_copy(staged, staged, guess_sem.at[place]).wait()

    @pl.when(gives_adjoint_guess)
    def _():
        pltpu.make_async_copy(returned, returned, back_out_sem.at[0]).wait()

    @pl.when(within > 0)
    def _():
        pltpu.make_async_copy(returned, returned, back_out_sem.at[0]).wait()

    @pl.loop(0, PASSES)
    def _(place):
        sent = outs.at[place]

        @pl.when(relays_fine(place) | relays_first(place) | relays_second(place))
        def _():
            pltpu.make_async_copy(sent, sent, out_sem.at[place]).wait()

        @pl.when(relays_first(place) | relays_second(place))
        def _():
            pltpu.make_async_copy(sent, sent, far_sem.at[place]).wait()

    for offset in range(1, copies):
        sender = lax.rem(replica + offset, copies)
        pltpu.make_async_copy(
            gain_parts.at[sender], gain_parts.at[sender], gain_in_sem.at[sender]
        ).wait()
        send_gain(offset).wait_send()
    grads[...] = jnp.sum(gain_parts[...], axis=0)
    for part in range(PARTS):
        write_states(part).wait()
    for part in range(BACK_PARTS):
        write_adjoints(part).wait()


def solution(mesh):
    depth = mesh.shape["layer"]
    copies = mesh.shape["dp"]

    def on_device(embedded, guess, qkv_weight, out_weight, norm_gain, cotangent, adjoint_guess):
        tokens, width = embedded.shape
        chunks = SEQ // ROWS
        anywhere = pl.BlockSpec(memory_space=pl.ANY)
        vector = pl.BlockSpec(memory_space=pltpu.VMEM)
        results = pl.pallas_call(
            functools.partial(kernel, depth, copies),
            out_shape=(
                pltpu.VMEM((1, tokens, width), F32),
                pltpu.VMEM((1, tokens, width), F32),
                pltpu.VMEM((1, width), F32),
            ),
            in_specs=[anywhere] * 7,
            out_specs=(vector,) * 3,
            scratch_shapes=[
                pltpu.VMEM((width, 3 * width), BF16),
                pltpu.VMEM((width, width), BF16),
                pltpu.VMEM((3 * width, width), BF16),
                pltpu.VMEM((width, width), BF16),
                pltpu.VMEM((1, width), F32),
                pltpu.VMEM((PASSES, PARTS, SEQ, width // PARTS), F32),
                pltpu.VMEM((PASSES, PARTS, SEQ, width // PARTS), F32),
                pltpu.VMEM((PARTS, SEQ, width // PARTS), F32),
                pltpu.VMEM((2, SEQ, 3 * width), BF16),
                pltpu.VMEM((HEADS, SEQ, SEQ), BF16),
                pltpu.VMEM((BACK_PARTS, SEQ, width // BACK_PARTS), F32),
                pltpu.VMEM((BACK_PARTS, SEQ, width // BACK_PARTS), F32),
                pltpu.VMEM((SEQ, width), BF16),
                pltpu.VMEM((SEQ, width), F32),
                pltpu.VMEM((copies, 1, width), F32),
                pltpu.SemaphoreType.DMA((PARTS + 1,)),
                pltpu.SemaphoreType.DMA((2,)),
                pltpu.SemaphoreType.DMA((PASSES, chunks, PARTS)),
                pltpu.SemaphoreType.DMA((PASSES,)),
                pltpu.SemaphoreType.DMA((PASSES,)),
                pltpu.SemaphoreType.DMA((2,)),
                pltpu.SemaphoreType.DMA((BACK_PARTS,)),
                pltpu.SemaphoreType.DMA((1,)),
                pltpu.SemaphoreType.DMA((copies,)),
                pltpu.SemaphoreType.DMA((copies,)),
                pltpu.SemaphoreType.DMA((PARTS + BACK_PARTS,)),
            ],
            compiler_params=pltpu.CompilerParams(
                collective_id=0, has_side_effects=True, vmem_limit_bytes=60 * 2**20
            ),
        )(embedded, guess, qkv_weight, out_weight, norm_gain, cotangent, adjoint_guess)
        return results

    return jax.shard_map(
        on_device,
        mesh=mesh,
        in_specs=(
            P("dp", None),
            P("layer", "dp", None),
            P("layer", None, None),
            P("layer", None, None),
            P("layer", None),
            P("dp", None),
            P("layer", "dp", None),
        ),
        out_specs=(P("layer", "dp", None), P("layer", "dp", None), P("layer", None)),
        check_vma=False,
    )
```

```python
import functools

import jax
import jax.numpy as jnp
from jax import lax
from jax.experimental import pallas as pl
from jax.experimental.pallas import tpu as pltpu
from jax.sharding import PartitionSpec as P

HEADS = 8
SEQ = 128
ROWS = 32
PARTS = 8
PASSES = 6
HALVES = 2
BACK_PARTS = 4
TURNS = 4

coarse_ratio = 4.0
norm_eps = 1e-06

F32 = jnp.float32
BF16 = jnp.bfloat16
MESH = pl.DeviceIdType.MESH


def dot(a, b):
    return jnp.dot(a, b, preferred_element_type=F32)


def dot_nt(a, b):
    return lax.dot_general(a, b, (((1,), (1,)), ((), ())), preferred_element_type=F32)


def dot_tn(a, b):
    return lax.dot_general(a, b, (((0,), (0,)), ((), ())), preferred_element_type=F32)


def kernel(
    depth,
    copies,
    embedded,
    guess,
    qkv_weight,
    out_weight,
    norm_gain,
    cotangent,
    adjoint_guess,
    states,
    adjoints,
    grads,
    w_qkv,
    w_out,
    w_qkv_t,
    w_out_t,
    gain,
    ins,
    outs,
    base,
    proj,
    probs,
    received,
    returned,
    d_context_ref,
    staged,
    gain_parts,
    weight_sem,
    load_sem,
    in_sem,
    out_sem,
    far_sem,
    guess_sem,
    back_in_sem,
    back_out_sem,
    gain_in_sem,
    gain_out_sem,
    final_sem,
):
    width = gain.shape[-1]
    head_dim = width // HEADS
    part_width = width // PARTS
    back_width = width // BACK_PARTS
    chunks = SEQ // ROWS
    groups = depth // 4
    me = lax.axis_index("layer")
    replica = lax.axis_index("dp")
    group = me // 4
    within = me % 4
    following = lax.rem(me + 1, depth)
    preceding = lax.rem(me + depth - 1, depth)
    far_on = lax.rem(me + 4, depth)
    far_back = lax.rem(me + depth - 4, depth)

    def rows_of(chunk):
        return pl.ds(pl.multiple_of(chunk * ROWS, ROWS), ROWS)

    def cols_of(part):
        return pl.ds(part * part_width, part_width)

    def load_qkv(part):
        return pltpu.make_async_copy(
            qkv_weight.at[0, cols_of(part)], w_qkv.at[cols_of(part)], weight_sem.at[part]
        )

    load_out = pltpu.make_async_copy(out_weight.at[0], w_out, weight_sem.at[PARTS])
    load_gain = pltpu.make_async_copy(norm_gain, gain, load_sem.at[0])
    load_guess = pltpu.make_async_copy(guess.at[0], staged, load_sem.at[1])
    gives_guess = (within == 3) & (group < groups - 1)
    gives_adjoint_guess = (within == 0) & (group > 0)
    for part in range(PARTS):
        load_qkv(part).start()
    load_out.start()
    load_gain.start()

    @pl.when(gives_guess)
    def _():
        load_guess.start()

    barrier = pltpu.get_barrier_semaphore()
    for neighbour in (following, preceding):
        pl.semaphore_signal(
            barrier, inc=1, device_id={"layer": neighbour}, device_id_type=MESH
        )
    for offset in range(1, copies):
        pl.semaphore_signal(
            barrier,
            inc=1,
            device_id={"dp": lax.rem(replica + offset, copies)},
            device_id_type=MESH,
        )

    @pl.when(within == 3)
    def _():
        for neighbour in (far_on, far_back):
            pl.semaphore_signal(
                barrier, inc=1, device_id={"layer": neighbour}, device_id_type=MESH
            )

    @pl.when(me == 0)
    def _():
        @pl.loop(0, chunks)
        def _(chunk):
            for part in range(PARTS):
                pltpu.make_async_copy(
                    embedded.at[rows_of(chunk), cols_of(part)],
                    ins.at[1, part, rows_of(chunk)],
                    in_sem.at[1, chunk, part],
                ).start()

    @pl.when(me == depth - 1)
    def _():
        for part in range(BACK_PARTS):
            pltpu.make_async_copy(
                cotangent.at[:, pl.ds(part * back_width, back_width)],
                received.at[part],
                back_in_sem.at[part],
            ).start()

    proj[...] = jnp.zeros_like(proj)

    @pl.when(me > 0)
    def _():
        pl.semaphore_wait(barrier, copies + 1 + 2 * (within // 3))

    def send_guess(chunk, part, place, target):
        return pltpu.make_async_remote_copy(
            src_ref=staged.at[rows_of(chunk), cols_of(part)],
            dst_ref=ins.at[place, part, rows_of(chunk)],
            send_sem=guess_sem.at[place],
            recv_sem=in_sem.at[place, chunk, part],
            device_id={"layer": target},
            device_id_type=MESH,
        )

    def send_adjoint_guess(part):
        return pltpu.make_async_remote_copy(
            src_ref=adjoint_guess.at[0, :, pl.ds(part * back_width, back_width)],
            dst_ref=received.at[part],
            send_sem=back_out_sem.at[0],
            recv_sem=back_in_sem.at[part],
            device_id={"layer": preceding},
            device_id_type=MESH,
        )

    @pl.when(gives_guess)
    def _():
        load_guess.wait()

        @pl.loop(0, chunks)
        def _(chunk):
            for part in range(PARTS):
                send_guess(chunk, part, 1, following).start()

        @pl.loop(0, chunks)
        def _(chunk):
            for part in range(PARTS):
                send_guess(chunk, part, 0, far_on).start()

    @pl.when(gives_adjoint_guess)
    def _():
        for part in range(BACK_PARTS):
            send_adjoint_guess(part).start()

    load_gain.wait()

    def is_active(place):
        needed = jnp.where(place == 0, 1, place // 2)
        return ((within == 3) | (place % 2 == 1)) & (group >= needed)

    def relays_fine(place):
        return is_active(place) & (within < 3)

    def relays_first(place):
        right = ((group == 0) & (place == 1)) | ((group >= 1) & (place == 2))
        return (within == 3) & (group < groups - 1) & right

    def relays_second(place):
        right = ((group == 1) & (place == 3)) | ((group >= 2) & (place == 4))
        return (within == 3) & (group < groups - 1) & right

    def send_main(place, chunk, part):
        second = relays_second(place)
        swapped = second & (group == groups - 2)
        fine = within < 3
        slot = jnp.where(second, 4, 2)
        target = jnp.where(fine | swapped, following, far_on)
        to_place = jnp.where(fine, place, jnp.where(swapped, slot + 1, slot))
        return pltpu.make_async_remote_copy(
            src_ref=outs.at[place, part, rows_of(chunk)],
            dst_ref=ins.at[to_place, part, rows_of(chunk)],
            send_sem=out_sem.at[place],
            recv_sem=in_sem.at[to_place, chunk, part],
            device_id={"layer": target},
            device_id_type=MESH,
        )

    def send_other(place, chunk, part):
        second = relays_second(place)
        swapped = second & (group == groups - 2)
        slot = jnp.where(second, 4, 2)
        target = jnp.where(swapped, far_on, following)
        to_place = jnp.where(swapped, slot, slot + 1)
        return pltpu.make_async_remote_copy(
            src_ref=outs.at[place, part, rows_of(chunk)],
            dst_ref=ins.at[to_place, part, rows_of(chunk)],
            send_sem=far_sem.at[place],
            recv_sem=in_sem.at[to_place, chunk, part],
            device_id={"layer": target},
            device_id_type=MESH,
        )

    half_cols = [
        slice(half * (width // HALVES), (half + 1) * (width // HALVES)) for half in range(HALVES)
    ]
    causal_cols = lax.broadcasted_iota(jnp.int32, (ROWS, SEQ), 1)
    causal_rows = lax.broadcasted_iota(jnp.int32, (ROWS, SEQ), 0)
    scale = head_dim**-0.5

    def mix_parts(streams):
        total = None
        for part in range(PARTS):
            cols = cols_of(part)
            for place, chunk, _ in streams:
                pltpu.make_async_copy(
                    ins.at[place, part, rows_of(chunk)],
                    ins.at[place, part, rows_of(chunk)],
                    in_sem.at[place, chunk, part],
                ).wait()
            stream = jnp.concatenate(
                [ins[place, part, rows_of(chunk), :] for place, chunk, _ in streams], axis=0
            )
            square = jnp.sum(stream * stream, axis=-1, keepdims=True)
            product = dot((stream * gain[:, cols]).astype(BF16), w_qkv[cols, :])
            if total is None:
                total, squares = product, square
            else:
                total, squares = total + product, squares + square
        root = lax.rsqrt(squares * (1.0 / width) + norm_eps)
        projected = (total * root).astype(BF16)
        pieces = [projected[i * ROWS : (i + 1) * ROWS] for i in range(len(streams))]
        for piece, (_, chunk, which) in zip(pieces, streams):
            proj[which, rows_of(chunk), :] = piece
        work = [
            (piece, chunk, which, head * head_dim)
            for piece, (_, chunk, which) in zip(pieces, streams)
            for head in range(HEADS)
        ]
        scores = []
        for piece, chunk, which, first_col in work:
            causal = causal_rows + chunk * ROWS >= causal_cols
            query = piece[:, first_col : first_col + head_dim]
            key = proj[which, :, width + first_col : width + first_col + head_dim]
            scores.append(jnp.where(causal, dot_nt(query, key) * scale, -1e30))
        exps = [jnp.exp(s - jnp.max(s, axis=-1, keepdims=True)) for s in scores]
        inverses = [1.0 / jnp.sum(e, axis=-1, keepdims=True) for e in exps]
        mixed = []
        for (_, _, which, first_col), e, inverse in zip(work, exps, inverses):
            value = proj[which, :, 2 * width + first_col : 2 * width + first_col + head_dim]
            mixed.append((dot(e.astype(BF16), value) * inverse).astype(BF16))
        contexts = [
            jnp.concatenate(mixed[i * HEADS : (i + 1) * HEADS], axis=1)
            for i in range(len(streams))
        ]
        return jnp.concatenate(contexts, axis=0), exps, inverses

    def keep_probs(exps, inverses, chunk):
        for head in range(HEADS):
            probs[head, rows_of(chunk), :] = (exps[head] * inverses[head]).astype(BF16)

    def send_others(place, chunk):
        @pl.when(relays_first(place) | relays_second(place))
        def _():
            for part in range(PARTS):
                send_other(place, chunk, part).start()

    def one_pass(place, chunk):
        rows = rows_of(chunk)
        context, exps, inverses = mix_parts(((place, chunk, place % 2),))

        @pl.when(place == 0)
        def _():
            mix = dot(context, w_out[...])
            for part in range(PARTS):
                cols = slice(part * part_width, (part + 1) * part_width)
                base[part, rows, :] = -(ins[place, part, rows, :] + coarse_ratio * mix[:, cols])

        @pl.when((within < 3) | (group == 0))
        def _():
            halves = [dot(context, w_out[:, cols]) for cols in half_cols]

            @pl.when((me == 0) & (chunk == 0))
            def _():
                pl.semaphore_wait(barrier, copies + 1)

            for half, mix in enumerate(halves):
                for step in range(PARTS // HALVES):
                    part = half * (PARTS // HALVES) + step
                    cols = slice(step * part_width, (step + 1) * part_width)
                    outs[place, part, rows, :] = ins[place, part, rows, :] + mix[:, cols]
                for step in range(PARTS // HALVES):
                    send_main(place, chunk, half * (PARTS // HALVES) + step).start()
            send_others(place, chunk)

        keep_probs(exps, inverses, chunk)

    def transpose_weights():
        w_out_t[...] = w_out[...].T

        @pl.loop(0, 3 * TURNS)
        def _(block):
            turn_width = width // TURNS
            cols = pl.ds(pl.multiple_of(block * turn_width, turn_width), turn_width)
            w_qkv_t[cols, :] = w_qkv[:, cols].T

    def pull_known():
        for part in range(BACK_PARTS):
            pltpu.make_async_copy(received.at[part], received.at[part], back_in_sem.at[part]).wait()
        known = jnp.concatenate([received[part] for part in range(BACK_PARTS)], axis=1)
        d_context_ref[...] = dot(known.astype(BF16), w_out_t[...]).astype(BF16)

    def two_passes(place, chunk, paired):
        other_place = jnp.where(paired, place + 1, place)
        other_chunk = jnp.where(paired, chunk, chunk + 1)
        rows = rows_of(chunk)
        other_rows = rows_of(other_chunk)
        context, exps, inverses = mix_parts(
            ((place, chunk, 1), (other_place, other_chunk, jnp.where(paired, 0, 1)))
        )
        mix = dot(context, w_out[...])

        @pl.when(paired)
        def _():
            for part in range(PARTS):
                cols = slice(part * part_width, (part + 1) * part_width)
                end = base[part, rows, :] + (ins[place, part, rows, :] + mix[:ROWS, cols])
                step = ins[other_place, part, rows, :] + coarse_ratio * mix[ROWS:, cols]
                outs[other_place, part, rows, :] = end + step
                base[part, rows, :] = -step

        @pl.when(jnp.logical_not(paired))
        def _():
            for part in range(PARTS):
                cols = slice(part * part_width, (part + 1) * part_width)
                outs[place, part, rows, :] = ins[place, part, rows, :] + mix[:ROWS, cols]
                outs[place, part, other_rows, :] = (
                    ins[place, part, other_rows, :] + mix[ROWS:, cols]
                )
            for part in range(PARTS):
                send_main(place, chunk, part).start()

        @pl.when(relays_first(other_place) | relays_second(other_place))
        def _():
            for part in range(PARTS):
                send_main(other_place, other_chunk, part).start()

        @pl.when(jnp.logical_not(paired))
        def _():
            keep_probs(exps[:HEADS], inverses[:HEADS], chunk)
            keep_probs(exps[HEADS:], inverses[HEADS:], other_chunk)

            @pl.when(other_chunk == chunks - 1)
            def _():
                @pl.loop(0, chunks)
                def _(late_chunk):
                    send_others(place, late_chunk)

        @pl.when(paired)
        def _():
            send_others(other_place, other_chunk)

    def one_task(task, carry):
        turn = task // chunks
        chunk = task % chunks
        place = turn + turn // 2 + turn // 3
        ends = within == 3
        paired = ends & (((group >= 1) & (place == 1)) | ((group >= 2) & (place == 3)))
        joined = ends & (group == 1) & (place == 3)
        early = ends & (group > 0)

        @pl.when((early & (task == 0)) | (jnp.logical_not(early) & (task == 2 * chunks)))
        def _():
            transpose_weights()

        @pl.when(ends & (group >= 2) & (task == 3 * chunks))
        def _():
            pull_known()

        @pl.when(is_active(place) & jnp.logical_not(paired | joined))
        def _():
            one_pass(place, chunk)

        @pl.when(paired | (joined & (chunk % 2 == 0)))
        def _():
            two_passes(place, chunk, paired)

        return carry

    for part in range(PARTS):
        load_qkv(part).wait()
    load_out.wait()
    lax.fori_loop(0, 4 * chunks, one_task, 0)

    latest = 1 + 2 * jnp.minimum(group, 2)
    final = latest - jnp.where((within == 3) & (group >= 2), 1, 0)

    def write_states(part):
        return pltpu.make_async_copy(
            outs.at[final, part], states.at[0, :, cols_of(part)], final_sem.at[part]
        )

    for part in range(PARTS):
        write_states(part).start()

    def send_back(part):
        return pltpu.make_async_remote_copy(
            src_ref=returned.at[part],
            dst_ref=received.at[part],
            send_sem=back_out_sem.at[0],
            recv_sem=back_in_sem.at[part],
            device_id={"layer": preceding},
            device_id_type=MESH,
        )

    @pl.when((within == 3) & (group < 2))
    def _():
        pull_known()

    @pl.when(within < 3)
    def _():
        total = None
        for part in range(BACK_PARTS):
            pltpu.make_async_copy(received.at[part], received.at[part], back_in_sem.at[part]).wait()
            cols = slice(part * back_width, (part + 1) * back_width)
            product = dot(received[part].astype(BF16), w_out_t[cols, :])
            total = product if total is None else total + product
        d_context_ref[...] = total.astype(BF16)

    d_context = d_context_ref[...]
    heads = [slice(head * head_dim, (head + 1) * head_dim) for head in range(HEADS)]

    def kind(number, head):
        return slice(number * width + head * head_dim, number * width + (head + 1) * head_dim)

    d_probs = [dot_nt(d_context[:, heads[h]], proj[1, :, kind(2, h)]) for h in range(HEADS)]
    wides = [probs[h].astype(F32) for h in range(HEADS)]
    weighted = [d * p for d, p in zip(d_probs, wides)]
    inners = [jnp.sum(w, axis=-1, keepdims=True) for w in weighted]
    d_scores = [
        ((w - p * n) * scale).astype(BF16) for w, p, n in zip(weighted, wides, inners)
    ]
    d_query = [dot(d_scores[h], proj[1, :, kind(1, h)]).astype(BF16) for h in range(HEADS)]
    d_key = [dot_tn(d_scores[h], proj[1, :, kind(0, h)]).astype(BF16) for h in range(HEADS)]
    d_value = [dot_tn(probs[h], d_context[:, heads[h]]).astype(BF16) for h in range(HEADS)]
    d_normed = dot(jnp.concatenate(d_query + d_key + d_value, axis=1), w_qkv_t[...])
    stream = jnp.concatenate([ins[latest, part] for part in range(PARTS)], axis=1)
    square = jnp.sum(stream * stream, axis=-1, keepdims=True) * (1.0 / width)
    root = lax.rsqrt(square + norm_eps)
    unit = stream * root
    d_unit = d_normed * gain[...]
    slope = jnp.sum(d_unit * unit, axis=-1, keepdims=True) * (1.0 / width)
    pulled = root * (d_unit - unit * slope)

    @pl.when(within > 0)
    def _():
        for part in range(BACK_PARTS):
            cols = slice(part * back_width, (part + 1) * back_width)
            returned[part] = received[part] + pulled[:, cols]
            send_back(part).start()

    @pl.when(within == 0)
    def _():
        for part in range(BACK_PARTS):
            cols = slice(part * back_width, (part + 1) * back_width)
            returned[part] = received[part] + pulled[:, cols]

    gain_parts[replica] = jnp.sum(d_normed * unit, axis=0, keepdims=True)

    def send_gain(offset):
        return pltpu.make_async_remote_copy(
            src_ref=gain_parts.at[replica],
            dst_ref=gain_parts.at[replica],
            send_sem=gain_out_sem.at[offset],
            recv_sem=gain_in_sem.at[replica],
            device_id={"dp": lax.rem(replica + offset, copies)},
            device_id_type=MESH,
        )

    for offset in range(1, copies):
        send_gain(offset).start()

    def write_adjoints(part):
        return pltpu.make_async_copy(
            returned.at[part],
            adjoints.at[0, :, pl.ds(part * back_width, back_width)],
            final_sem.at[PARTS + part],
        )

    for part in range(BACK_PARTS):
        write_adjoints(part).start()

    @pl.when(gives_guess)
    def _():
        for place in range(2):
            pltpu.make_async_copy(staged, staged, guess_sem.at[place]).wait()

    @pl.when(gives_adjoint_guess)
    def _():
        pltpu.make_async_copy(returned, returned, back_out_sem.at[0]).wait()

    @pl.when(within > 0)
    def _():
        pltpu.make_async_copy(returned, returned, back_out_sem.at[0]).wait()

    @pl.loop(0, PASSES)
    def _(place):
        sent = outs.at[place]

        @pl.when(relays_fine(place) | relays_first(place) | relays_second(place))
        def _():
            pltpu.make_async_copy(sent, sent, out_sem.at[place]).wait()

        @pl.when(relays_first(place) | relays_second(place))
        def _():
            pltpu.make_async_copy(sent, sent, far_sem.at[place]).wait()

    for offset in range(1, copies):
        sender = lax.rem(replica + offset, copies)
        pltpu.make_async_copy(
            gain_parts.at[sender], gain_parts.at[sender], gain_in_sem.at[sender]
        ).wait()
        send_gain(offset).wait_send()
    grads[...] = jnp.sum(gain_parts[...], axis=0)
    for part in range(PARTS):
        write_states(part).wait()
    for part in range(BACK_PARTS):
        write_adjoints(part).wait()


def write_out(states_in, adjoints_in, grads_in, states, adjoints, grads, sems):
    pairs = ((states_in, states), (adjoints_in, adjoints), (grads_in, grads))
    moves = [
        pltpu.make_async_copy(source, target, sems.at[index])
        for index, (source, target) in enumerate(pairs)
    ]
    for move in moves:
        move.start()
    for move in moves:
        move.wait()


def solution(mesh):
    depth = mesh.shape["layer"]
    copies = mesh.shape["dp"]

    def on_device(embedded, guess, qkv_weight, out_weight, norm_gain, cotangent, adjoint_guess):
        tokens, width = embedded.shape
        chunks = SEQ // ROWS
        anywhere = pl.BlockSpec(memory_space=pl.ANY)
        vector = pl.BlockSpec(memory_space=pltpu.VMEM)
        results = pl.pallas_call(
            functools.partial(kernel, depth, copies),
            out_shape=(
                pltpu.VMEM((1, tokens, width), F32),
                pltpu.VMEM((1, tokens, width), F32),
                pltpu.VMEM((1, width), F32),
            ),
            in_specs=[anywhere] * 7,
            out_specs=(vector,) * 3,
            scratch_shapes=[
                pltpu.VMEM((width, 3 * width), BF16),
                pltpu.VMEM((width, width), BF16),
                pltpu.VMEM((3 * width, width), BF16),
                pltpu.VMEM((width, width), BF16),
                pltpu.VMEM((1, width), F32),
                pltpu.VMEM((PASSES, PARTS, SEQ, width // PARTS), F32),
                pltpu.VMEM((PASSES, PARTS, SEQ, width // PARTS), F32),
                pltpu.VMEM((PARTS, SEQ, width // PARTS), F32),
                pltpu.VMEM((2, SEQ, 3 * width), BF16),
                pltpu.VMEM((HEADS, SEQ, SEQ), BF16),
                pltpu.VMEM((BACK_PARTS, SEQ, width // BACK_PARTS), F32),
                pltpu.VMEM((BACK_PARTS, SEQ, width // BACK_PARTS), F32),
                pltpu.VMEM((SEQ, width), BF16),
                pltpu.VMEM((SEQ, width), F32),
                pltpu.VMEM((copies, 1, width), F32),
                pltpu.SemaphoreType.DMA((PARTS + 1,)),
                pltpu.SemaphoreType.DMA((2,)),
                pltpu.SemaphoreType.DMA((PASSES, chunks, PARTS)),
                pltpu.SemaphoreType.DMA((PASSES,)),
                pltpu.SemaphoreType.DMA((PASSES,)),
                pltpu.SemaphoreType.DMA((2,)),
                pltpu.SemaphoreType.DMA((BACK_PARTS,)),
                pltpu.SemaphoreType.DMA((1,)),
                pltpu.SemaphoreType.DMA((copies,)),
                pltpu.SemaphoreType.DMA((copies,)),
                pltpu.SemaphoreType.DMA((PARTS + BACK_PARTS,)),
            ],
            compiler_params=pltpu.CompilerParams(
                collective_id=0, has_side_effects=True, vmem_limit_bytes=60 * 2**20
            ),
        )(embedded, guess, qkv_weight, out_weight, norm_gain, cotangent, adjoint_guess)
        results = tuple(pltpu.with_memory_space_constraint(r, pltpu.VMEM) for r in results)
        return pl.pallas_call(
            write_out,
            out_shape=tuple(jax.ShapeDtypeStruct(r.shape, r.dtype) for r in results),
            in_specs=[vector] * 3,
            out_specs=(anywhere,) * 3,
            scratch_shapes=[pltpu.SemaphoreType.DMA((3,))],
        )(*results)

    return jax.shard_map(
        on_device,
        mesh=mesh,
        in_specs=(
            P("dp", None),
            P("layer", "dp", None),
            P("layer", None, None),
            P("layer", None, None),
            P("layer", None),
            P("dp", None),
            P("layer", "dp", None),
        ),
        out_specs=(P("layer", "dp", None), P("layer", "dp", None), P("layer", None)),
        check_vma=False,
    )
```

```python
import functools

import jax
import jax.numpy as jnp
from jax import lax
from jax.experimental import pallas as pl
from jax.experimental.pallas import tpu as pltpu
from jax.sharding import PartitionSpec as P

HEADS = 8
SEQ = 128
ROWS = 32
PARTS = 8
PASSES = 6
HALVES = 2
BACK_PARTS = 4
TURNS = 4

coarse_ratio = 4.0
norm_eps = 1e-06

F32 = jnp.float32
BF16 = jnp.bfloat16
MESH = pl.DeviceIdType.MESH


def dot(a, b):
    return jnp.dot(a, b, preferred_element_type=F32)


def dot_nt(a, b):
    return lax.dot_general(a, b, (((1,), (1,)), ((), ())), preferred_element_type=F32)


def dot_tn(a, b):
    return lax.dot_general(a, b, (((0,), (0,)), ((), ())), preferred_element_type=F32)


def kernel(
    depth,
    copies,
    embedded,
    guess,
    qkv_weight,
    out_weight,
    norm_gain,
    cotangent,
    adjoint_guess,
    states,
    adjoints,
    grads,
    w_qkv,
    w_out,
    w_qkv_t,
    w_out_t,
    gain,
    ins,
    outs,
    base,
    proj,
    probs,
    received,
    returned,
    d_context_ref,
    staged,
    gain_parts,
    weight_sem,
    load_sem,
    in_sem,
    out_sem,
    far_sem,
    guess_sem,
    back_in_sem,
    back_out_sem,
    gain_in_sem,
    gain_out_sem,
    final_sem,
):
    width = gain.shape[-1]
    head_dim = width // HEADS
    part_width = width // PARTS
    back_width = width // BACK_PARTS
    chunks = SEQ // ROWS
    groups = depth // 4
    me = lax.axis_index("layer")
    replica = lax.axis_index("dp")
    group = me // 4
    within = me % 4
    following = lax.rem(me + 1, depth)
    preceding = lax.rem(me + depth - 1, depth)
    far_on = lax.rem(me + 4, depth)
    far_back = lax.rem(me + depth - 4, depth)

    def rows_of(chunk):
        return pl.ds(pl.multiple_of(chunk * ROWS, ROWS), ROWS)

    def cols_of(part):
        return pl.ds(part * part_width, part_width)

    def load_qkv(part):
        return pltpu.make_async_copy(
            qkv_weight.at[0, cols_of(part)], w_qkv.at[cols_of(part)], weight_sem.at[part]
        )

    load_out = pltpu.make_async_copy(out_weight.at[0], w_out, weight_sem.at[PARTS])
    load_gain = pltpu.make_async_copy(norm_gain, gain, load_sem.at[0])
    load_guess = pltpu.make_async_copy(guess.at[0], staged, load_sem.at[1])
    gives_guess = (within == 3) & (group < groups - 1)
    gives_adjoint_guess = (within == 0) & (group > 0)
    @pl.when(me == 0)
    def _():
        @pl.loop(0, chunks)
        def _(chunk):
            for part in range(PARTS):
                pltpu.make_async_copy(
                    embedded.at[rows_of(chunk), cols_of(part)],
                    ins.at[1, part, rows_of(chunk)],
                    in_sem.at[1, chunk, part],
                ).start()

    load_gain.start()
    for part in range(PARTS):
        load_qkv(part).start()
    load_out.start()

    @pl.when(gives_guess)
    def _():
        load_guess.start()

    barrier = pltpu.get_barrier_semaphore()
    for neighbour in (following, preceding):
        pl.semaphore_signal(
            barrier, inc=1, device_id={"layer": neighbour}, device_id_type=MESH
        )
    for offset in range(1, copies):
        pl.semaphore_signal(
            barrier,
            inc=1,
            device_id={"dp": lax.rem(replica + offset, copies)},
            device_id_type=MESH,
        )

    @pl.when(within == 3)
    def _():
        for neighbour in (far_on, far_back):
            pl.semaphore_signal(
                barrier, inc=1, device_id={"layer": neighbour}, device_id_type=MESH
            )

    @pl.when(me == depth - 1)
    def _():
        for part in range(BACK_PARTS):
            pltpu.make_async_copy(
                cotangent.at[:, pl.ds(part * back_width, back_width)],
                received.at[part],
                back_in_sem.at[part],
            ).start()

    proj[...] = jnp.zeros_like(proj)

    @pl.when(me > 0)
    def _():
        pl.semaphore_wait(barrier, copies + 1 + 2 * (within // 3))

    def send_guess(chunk, part, place, target):
        return pltpu.make_async_remote_copy(
            src_ref=staged.at[rows_of(chunk), cols_of(part)],
            dst_ref=ins.at[place, part, rows_of(chunk)],
            send_sem=guess_sem.at[place],
            recv_sem=in_sem.at[place, chunk, part],
            device_id={"layer": target},
            device_id_type=MESH,
        )

    def send_adjoint_guess(part):
        return pltpu.make_async_remote_copy(
            src_ref=adjoint_guess.at[0, :, pl.ds(part * back_width, back_width)],
            dst_ref=received.at[part],
            send_sem=back_out_sem.at[0],
            recv_sem=back_in_sem.at[part],
            device_id={"layer": preceding},
            device_id_type=MESH,
        )

    @pl.when(gives_guess)
    def _():
        load_guess.wait()

        @pl.loop(0, chunks)
        def _(chunk):
            for part in range(PARTS):
                send_guess(chunk, part, 1, following).start()

        @pl.loop(0, chunks)
        def _(chunk):
            for part in range(PARTS):
                send_guess(chunk, part, 0, far_on).start()

    @pl.when(gives_adjoint_guess)
    def _():
        for part in range(BACK_PARTS):
            send_adjoint_guess(part).start()

    load_gain.wait()

    def is_active(place):
        needed = jnp.where(place == 0, 1, place // 2)
        return ((within == 3) | (place % 2 == 1)) & (group >= needed)

    def relays_fine(place):
        return is_active(place) & (within < 3)

    def relays_first(place):
        right = ((group == 0) & (place == 1)) | ((group >= 1) & (place == 2))
        return (within == 3) & (group < groups - 1) & right

    def relays_second(place):
        right = ((group == 1) & (place == 3)) | ((group >= 2) & (place == 4))
        return (within == 3) & (group < groups - 1) & right

    def send_main(place, chunk, part):
        second = relays_second(place)
        swapped = second & (group == groups - 2)
        fine = within < 3
        slot = jnp.where(second, 4, 2)
        target = jnp.where(fine | swapped, following, far_on)
        to_place = jnp.where(fine, place, jnp.where(swapped, slot + 1, slot))
        return pltpu.make_async_remote_copy(
            src_ref=outs.at[place, part, rows_of(chunk)],
            dst_ref=ins.at[to_place, part, rows_of(chunk)],
            send_sem=out_sem.at[place],
            recv_sem=in_sem.at[to_place, chunk, part],
            device_id={"layer": target},
            device_id_type=MESH,
        )

    def send_other(place, chunk, part):
        second = relays_second(place)
        swapped = second & (group == groups - 2)
        slot = jnp.where(second, 4, 2)
        target = jnp.where(swapped, far_on, following)
        to_place = jnp.where(swapped, slot, slot + 1)
        return pltpu.make_async_remote_copy(
            src_ref=outs.at[place, part, rows_of(chunk)],
            dst_ref=ins.at[to_place, part, rows_of(chunk)],
            send_sem=far_sem.at[place],
            recv_sem=in_sem.at[to_place, chunk, part],
            device_id={"layer": target},
            device_id_type=MESH,
        )

    half_cols = [
        slice(half * (width // HALVES), (half + 1) * (width // HALVES)) for half in range(HALVES)
    ]
    causal_cols = lax.broadcasted_iota(jnp.int32, (ROWS, SEQ), 1)
    causal_rows = lax.broadcasted_iota(jnp.int32, (ROWS, SEQ), 0)
    scale = head_dim**-0.5

    def mix_parts(streams):
        total = None
        for part in range(PARTS):
            cols = cols_of(part)
            for place, chunk, _ in streams:
                pltpu.make_async_copy(
                    ins.at[place, part, rows_of(chunk)],
                    ins.at[place, part, rows_of(chunk)],
                    in_sem.at[place, chunk, part],
                ).wait()
            stream = jnp.concatenate(
                [ins[place, part, rows_of(chunk), :] for place, chunk, _ in streams], axis=0
            )
            square = jnp.sum(stream * stream, axis=-1, keepdims=True)
            product = dot((stream * gain[:, cols]).astype(BF16), w_qkv[cols, :])
            if total is None:
                total, squares = product, square
            else:
                total, squares = total + product, squares + square
        root = lax.rsqrt(squares * (1.0 / width) + norm_eps)
        projected = (total * root).astype(BF16)
        pieces = [projected[i * ROWS : (i + 1) * ROWS] for i in range(len(streams))]
        for piece, (_, chunk, which) in zip(pieces, streams):
            proj[which, rows_of(chunk), :] = piece
        work = [
            (piece, chunk, which, head * head_dim)
            for piece, (_, chunk, which) in zip(pieces, streams)
            for head in range(HEADS)
        ]
        scores = []
        for piece, chunk, which, first_col in work:
            causal = causal_rows + chunk * ROWS >= causal_cols
            query = piece[:, first_col : first_col + head_dim]
            key = proj[which, :, width + first_col : width + first_col + head_dim]
            scores.append(jnp.where(causal, dot_nt(query, key) * scale, -1e30))
        exps = [jnp.exp(s - jnp.max(s, axis=-1, keepdims=True)) for s in scores]
        inverses = [1.0 / jnp.sum(e, axis=-1, keepdims=True) for e in exps]
        mixed = []
        for (_, _, which, first_col), e, inverse in zip(work, exps, inverses):
            value = proj[which, :, 2 * width + first_col : 2 * width + first_col + head_dim]
            mixed.append((dot(e.astype(BF16), value) * inverse).astype(BF16))
        contexts = [
            jnp.concatenate(mixed[i * HEADS : (i + 1) * HEADS], axis=1)
            for i in range(len(streams))
        ]
        return jnp.concatenate(contexts, axis=0), exps, inverses

    def keep_probs(exps, inverses, chunk):
        for head in range(HEADS):
            probs[head, rows_of(chunk), :] = (exps[head] * inverses[head]).astype(BF16)

    def send_others(place, chunk):
        @pl.when(relays_first(place) | relays_second(place))
        def _():
            for part in range(PARTS):
                send_other(place, chunk, part).start()

    def one_pass(place, chunk):
        rows = rows_of(chunk)
        context, exps, inverses = mix_parts(((place, chunk, place % 2),))

        @pl.when(place == 0)
        def _():
            mix = dot(context, w_out[...])
            for part in range(PARTS):
                cols = slice(part * part_width, (part + 1) * part_width)
                base[part, rows, :] = -(ins[place, part, rows, :] + coarse_ratio * mix[:, cols])

        @pl.when((within < 3) | (group == 0))
        def _():
            opening = (me == 0) & (chunk == 0)

            @pl.when(opening)
            def _():
                load_out.wait()

            halves = [dot(context, w_out[:, cols]) for cols in half_cols]

            @pl.when(opening)
            def _():
                pl.semaphore_wait(barrier, copies + 1)

            for half, mix in enumerate(halves):
                for step in range(PARTS // HALVES):
                    part = half * (PARTS // HALVES) + step
                    cols = slice(step * part_width, (step + 1) * part_width)
                    outs[place, part, rows, :] = ins[place, part, rows, :] + mix[:, cols]
                for step in range(PARTS // HALVES):
                    send_main(place, chunk, half * (PARTS // HALVES) + step).start()
            send_others(place, chunk)

        keep_probs(exps, inverses, chunk)

    def transpose_weights():
        w_out_t[...] = w_out[...].T

        @pl.loop(0, 3 * TURNS)
        def _(block):
            turn_width = width // TURNS
            cols = pl.ds(pl.multiple_of(block * turn_width, turn_width), turn_width)
            w_qkv_t[cols, :] = w_qkv[:, cols].T

    def pull_known():
        for part in range(BACK_PARTS):
            pltpu.make_async_copy(received.at[part], received.at[part], back_in_sem.at[part]).wait()
        known = jnp.concatenate([received[part] for part in range(BACK_PARTS)], axis=1)
        d_context_ref[...] = dot(known.astype(BF16), w_out_t[...]).astype(BF16)

    def two_passes(place, chunk, paired):
        other_place = jnp.where(paired, place + 1, place)
        other_chunk = jnp.where(paired, chunk, chunk + 1)
        rows = rows_of(chunk)
        other_rows = rows_of(other_chunk)
        context, exps, inverses = mix_parts(
            ((place, chunk, 1), (other_place, other_chunk, jnp.where(paired, 0, 1)))
        )
        relayed = relays_first(other_place) | relays_second(other_place)

        def add_pair(part, cols, mix):
            end = base[part, rows, :] + (ins[place, part, rows, :] + mix[:ROWS, cols])
            step = ins[other_place, part, rows, :] + coarse_ratio * mix[ROWS:, cols]
            outs[other_place, part, rows, :] = end + step
            base[part, rows, :] = -step

        @pl.when(paired & relayed)
        def _():
            halves = [dot(context, w_out[:, cols]) for cols in half_cols]
            for half, mix in enumerate(halves):
                for step in range(PARTS // HALVES):
                    cols = slice(step * part_width, (step + 1) * part_width)
                    add_pair(half * (PARTS // HALVES) + step, cols, mix)
                for step in range(PARTS // HALVES):
                    part = half * (PARTS // HALVES) + step
                    send_main(other_place, other_chunk, part).start()
            send_others(other_place, other_chunk)

        @pl.when(paired & jnp.logical_not(relayed))
        def _():
            mix = dot(context, w_out[...])
            for part in range(PARTS):
                add_pair(part, slice(part * part_width, (part + 1) * part_width), mix)

        @pl.when(jnp.logical_not(paired))
        def _():
            mix = dot(context, w_out[...])
            for part in range(PARTS):
                cols = slice(part * part_width, (part + 1) * part_width)
                outs[place, part, rows, :] = ins[place, part, rows, :] + mix[:ROWS, cols]
                outs[place, part, other_rows, :] = (
                    ins[place, part, other_rows, :] + mix[ROWS:, cols]
                )
            for part in range(PARTS):
                send_main(place, chunk, part).start()

            for part in range(PARTS):
                send_main(other_place, other_chunk, part).start()
            keep_probs(exps[:HEADS], inverses[:HEADS], chunk)
            keep_probs(exps[HEADS:], inverses[HEADS:], other_chunk)

            @pl.when(other_chunk == chunks - 1)
            def _():
                @pl.loop(0, chunks)
                def _(late_chunk):
                    send_others(place, late_chunk)

    def one_task(task, carry):
        turn = task // chunks
        chunk = task % chunks
        place = turn + turn // 2 + turn // 3
        ends = within == 3
        paired = ends & (((group >= 1) & (place == 1)) | ((group >= 2) & (place == 3)))
        joined = ends & (group == 1) & (place == 3)
        early = ends & (group > 0)

        @pl.when((early & (task == 0)) | (jnp.logical_not(early) & (task == 2 * chunks)))
        def _():
            transpose_weights()

        @pl.when(ends & (group >= 2) & (task == 3 * chunks))
        def _():
            pull_known()

        @pl.when(is_active(place) & jnp.logical_not(paired | joined))
        def _():
            one_pass(place, chunk)

        @pl.when(paired | (joined & (chunk % 2 == 0)))
        def _():
            two_passes(place, chunk, paired)

        return carry

    for part in range(PARTS):
        load_qkv(part).wait()

    @pl.when(me > 0)
    def _():
        load_out.wait()

    lax.fori_loop(0, 4 * chunks, one_task, 0)

    latest = 1 + 2 * jnp.minimum(group, 2)
    final = latest - jnp.where((within == 3) & (group >= 2), 1, 0)

    def write_states(part):
        return pltpu.make_async_copy(
            outs.at[final, part], states.at[0, :, cols_of(part)], final_sem.at[part]
        )

    for part in range(PARTS):
        write_states(part).start()

    def send_back(part):
        return pltpu.make_async_remote_copy(
            src_ref=returned.at[part],
            dst_ref=received.at[part],
            send_sem=back_out_sem.at[0],
            recv_sem=back_in_sem.at[part],
            device_id={"layer": preceding},
            device_id_type=MESH,
        )

    @pl.when((within == 3) & (group < 2))
    def _():
        pull_known()

    @pl.when(within < 3)
    def _():
        total = None
        for part in range(BACK_PARTS):
            pltpu.make_async_copy(received.at[part], received.at[part], back_in_sem.at[part]).wait()
            cols = slice(part * back_width, (part + 1) * back_width)
            product = dot(received[part].astype(BF16), w_out_t[cols, :])
            total = product if total is None else total + product
        d_context_ref[...] = total.astype(BF16)

    d_context = d_context_ref[...]
    heads = [slice(head * head_dim, (head + 1) * head_dim) for head in range(HEADS)]

    def kind(number, head):
        return slice(number * width + head * head_dim, number * width + (head + 1) * head_dim)

    d_probs = [dot_nt(d_context[:, heads[h]], proj[1, :, kind(2, h)]) for h in range(HEADS)]
    wides = [probs[h].astype(F32) for h in range(HEADS)]
    weighted = [d * p for d, p in zip(d_probs, wides)]
    inners = [jnp.sum(w, axis=-1, keepdims=True) for w in weighted]
    d_scores = [
        ((w - p * n) * scale).astype(BF16) for w, p, n in zip(weighted, wides, inners)
    ]
    d_query = [dot(d_scores[h], proj[1, :, kind(1, h)]).astype(BF16) for h in range(HEADS)]
    d_key = [dot_tn(d_scores[h], proj[1, :, kind(0, h)]).astype(BF16) for h in range(HEADS)]
    d_value = [dot_tn(probs[h], d_context[:, heads[h]]).astype(BF16) for h in range(HEADS)]
    d_normed = dot(jnp.concatenate(d_query + d_key + d_value, axis=1), w_qkv_t[...])
    stream = jnp.concatenate([ins[latest, part] for part in range(PARTS)], axis=1)
    square = jnp.sum(stream * stream, axis=-1, keepdims=True) * (1.0 / width)
    root = lax.rsqrt(square + norm_eps)
    unit = stream * root

    def send_gain(offset):
        return pltpu.make_async_remote_copy(
            src_ref=gain_parts.at[replica],
            dst_ref=gain_parts.at[replica],
            send_sem=gain_out_sem.at[offset],
            recv_sem=gain_in_sem.at[replica],
            device_id={"dp": lax.rem(replica + offset, copies)},
            device_id_type=MESH,
        )

    def share_gain():
        gain_parts[replica] = jnp.sum(d_normed * unit, axis=0, keepdims=True)
        for offset in range(1, copies):
            send_gain(offset).start()

    @pl.when(within == 0)
    def _():
        share_gain()

    d_unit = d_normed * gain[...]
    slope = jnp.sum(d_unit * unit, axis=-1, keepdims=True) * (1.0 / width)
    pulled = root * (d_unit - unit * slope)

    @pl.when(within > 0)
    def _():
        for part in range(BACK_PARTS):
            cols = slice(part * back_width, (part + 1) * back_width)
            returned[part] = received[part] + pulled[:, cols]
            send_back(part).start()
        share_gain()

    @pl.when(within == 0)
    def _():
        for part in range(BACK_PARTS):
            cols = slice(part * back_width, (part + 1) * back_width)
            returned[part] = received[part] + pulled[:, cols]

    def write_adjoints(part):
        return pltpu.make_async_copy(
            returned.at[part],
            adjoints.at[0, :, pl.ds(part * back_width, back_width)],
            final_sem.at[PARTS + part],
        )

    for part in range(BACK_PARTS):
        write_adjoints(part).start()

    @pl.when(gives_guess)
    def _():
        for place in range(2):
            pltpu.make_async_copy(staged, staged, guess_sem.at[place]).wait()

    @pl.when(gives_adjoint_guess)
    def _():
        pltpu.make_async_copy(returned, returned, back_out_sem.at[0]).wait()

    @pl.when(within > 0)
    def _():
        pltpu.make_async_copy(returned, returned, back_out_sem.at[0]).wait()

    @pl.loop(0, PASSES)
    def _(place):
        sent = outs.at[place]

        @pl.when(relays_fine(place) | relays_first(place) | relays_second(place))
        def _():
            pltpu.make_async_copy(sent, sent, out_sem.at[place]).wait()

        @pl.when(relays_first(place) | relays_second(place))
        def _():
            pltpu.make_async_copy(sent, sent, far_sem.at[place]).wait()

    for offset in range(1, copies):
        sender = lax.rem(replica + offset, copies)
        pltpu.make_async_copy(
            gain_parts.at[sender], gain_parts.at[sender], gain_in_sem.at[sender]
        ).wait()
        send_gain(offset).wait_send()
    grads[...] = jnp.sum(gain_parts[...], axis=0)
    for part in range(PARTS):
        write_states(part).wait()
    for part in range(BACK_PARTS):
        write_adjoints(part).wait()


def write_out(states_in, adjoints_in, grads_in, states, adjoints, grads, sems):
    pairs = ((states_in, states), (adjoints_in, adjoints), (grads_in, grads))
    moves = [
        pltpu.make_async_copy(source, target, sems.at[index])
        for index, (source, target) in enumerate(pairs)
    ]
    for move in moves:
        move.start()
    for move in moves:
        move.wait()


def solution(mesh):
    depth = mesh.shape["layer"]
    copies = mesh.shape["dp"]

    def on_device(embedded, guess, qkv_weight, out_weight, norm_gain, cotangent, adjoint_guess):
        tokens, width = embedded.shape
        chunks = SEQ // ROWS
        anywhere = pl.BlockSpec(memory_space=pl.ANY)
        vector = pl.BlockSpec(memory_space=pltpu.VMEM)
        results = pl.pallas_call(
            functools.partial(kernel, depth, copies),
            out_shape=(
                pltpu.VMEM((1, tokens, width), F32),
                pltpu.VMEM((1, tokens, width), F32),
                pltpu.VMEM((1, width), F32),
            ),
            in_specs=[anywhere] * 7,
            out_specs=(vector,) * 3,
            scratch_shapes=[
                pltpu.VMEM((width, 3 * width), BF16),
                pltpu.VMEM((width, width), BF16),
                pltpu.VMEM((3 * width, width), BF16),
                pltpu.VMEM((width, width), BF16),
                pltpu.VMEM((1, width), F32),
                pltpu.VMEM((PASSES, PARTS, SEQ, width // PARTS), F32),
                pltpu.VMEM((PASSES, PARTS, SEQ, width // PARTS), F32),
                pltpu.VMEM((PARTS, SEQ, width // PARTS), F32),
                pltpu.VMEM((2, SEQ, 3 * width), BF16),
                pltpu.VMEM((HEADS, SEQ, SEQ), BF16),
                pltpu.VMEM((BACK_PARTS, SEQ, width // BACK_PARTS), F32),
                pltpu.VMEM((BACK_PARTS, SEQ, width // BACK_PARTS), F32),
                pltpu.VMEM((SEQ, width), BF16),
                pltpu.VMEM((SEQ, width), F32),
                pltpu.VMEM((copies, 1, width), F32),
                pltpu.SemaphoreType.DMA((PARTS + 1,)),
                pltpu.SemaphoreType.DMA((2,)),
                pltpu.SemaphoreType.DMA((PASSES, chunks, PARTS)),
                pltpu.SemaphoreType.DMA((PASSES,)),
                pltpu.SemaphoreType.DMA((PASSES,)),
                pltpu.SemaphoreType.DMA((2,)),
                pltpu.SemaphoreType.DMA((BACK_PARTS,)),
                pltpu.SemaphoreType.DMA((1,)),
                pltpu.SemaphoreType.DMA((copies,)),
                pltpu.SemaphoreType.DMA((copies,)),
                pltpu.SemaphoreType.DMA((PARTS + BACK_PARTS,)),
            ],
            compiler_params=pltpu.CompilerParams(
                collective_id=0, has_side_effects=True, vmem_limit_bytes=60 * 2**20
            ),
        )(embedded, guess, qkv_weight, out_weight, norm_gain, cotangent, adjoint_guess)
        results = tuple(pltpu.with_memory_space_constraint(r, pltpu.VMEM) for r in results)
        return pl.pallas_call(
            write_out,
            out_shape=tuple(jax.ShapeDtypeStruct(r.shape, r.dtype) for r in results),
            in_specs=[vector] * 3,
            out_specs=(anywhere,) * 3,
            scratch_shapes=[pltpu.SemaphoreType.DMA((3,))],
        )(*results)

    return jax.shard_map(
        on_device,
        mesh=mesh,
        in_specs=(
            P("dp", None),
            P("layer", "dp", None),
            P("layer", None, None),
            P("layer", None, None),
            P("layer", None),
            P("dp", None),
            P("layer", "dp", None),
        ),
        out_specs=(P("layer", "dp", None), P("layer", "dp", None), P("layer", None)),
        check_vma=False,
    )
```
